128 devices in a mesh: row: 16 (over z, x_hi, core), col: 8 (over y, x_lo).
Axes of the slice: x: 4 (x_hi: 2, x_lo: 2; x = x_hi * 2 + x_lo), y: 4, z: 4, core: 2. Of those that a mesh axis runs over, the one named last changes fastest.
Arguments:
- amplitudes: bfloat16 [512, 512, 256], P('row', 'col'), may hold values from -6 to 6
- integrals: bfloat16 [512, 512, 256], P('row', 'col'), may hold values from -0.0625 to 0.0625
- occ_energy: float32 [16], replicated, may hold values from -1.5 to -0.5
- vir_energy: float32 [512], replicated, may hold values from 0.5 to 3
Outputs:
- updated: float32 [512, 512, 256], P('row', 'col')
The draws below stay inside these ranges and needn't reach their ends.
All inputs are finite; a program needn't handle non-finite values.
Results may differ from the reference program's by a relative error of at most 0.0017.
Values may be sent and summed in bfloat16 or wider, within the bound.
A program may use at most 192 MiB of HBM per device.

```python
import jax
import jax.numpy as jnp
from jax import lax

VIRT = 512
OCC = 16


def level_of(own_key, shape, pieces, least, largest):
    level, own = 1.0, jax.random.fold_in(own_key, 6)
    for axis_at, parts in pieces:
        steps = jnp.exp(jax.random.uniform(jax.random.fold_in(own, axis_at), (parts,), jnp.float32, least / len(pieces), largest / len(pieces)))
        level = level * jnp.repeat(steps, shape[axis_at] // parts).reshape([-1 if axis == axis_at else 1 for axis in range(len(shape))])
    return level


def normal_values(own_key, dims, width, bound, cuts=(), dtype=jnp.bfloat16):
    level = level_of(own_key, dims, cuts, -0.22, 0.18) if cuts else 1.0
    values = jax.random.normal(own_key, dims, jnp.float32) * width * level
    return jnp.minimum(jnp.maximum(values, -bound), bound).astype(dtype)


def setup_inputs(seed: int = 0) -> dict:
    key_of = jax.random.split(jax.random.key(seed), 5)
    amplitudes = normal_values(key_of[0], (VIRT, VIRT, OCC * OCC), 1.0, 6.0, ((0, 16), (1, 8)))
    integrals = normal_values(key_of[1], (VIRT, VIRT, OCC * OCC), (VIRT * OCC) ** -0.5, 0.0625, ((0, 16), (1, 8)))
    occ_energy = jnp.clip(jax.random.uniform(key_of[2], (OCC,), jnp.float32, -1.5, -0.5), -1.5, -0.5)
    vir_energy = jnp.clip(jax.random.uniform(key_of[3], (VIRT,), jnp.float32, 0.5, 3.0), 0.5, 3.0)
    return {"amplitudes": amplitudes, "integrals": integrals, "occ_energy": occ_energy, "vir_energy": vir_energy}


def reference(amplitudes, integrals, occ_energy, vir_energy):
    amp_full = amplitudes.astype(jnp.float32).reshape(VIRT, VIRT, OCC, OCC)
    int_full = integrals.astype(jnp.float32).reshape(VIRT, VIRT, OCC, OCC)
    cycle_term = jnp.einsum("acik,cbkj->abij", amp_full, int_full, precision=lax.Precision.HIGHEST)
    antisym = cycle_term - cycle_term.transpose(0, 1, 3, 2)
    resid_term = antisym - antisym.transpose(1, 0, 2, 3)
    denominator = (occ_energy[None, None, :, None] + occ_energy[None, None, None, :]
                   - vir_energy[:, None, None, None] - vir_energy[None, :, None, None])
    result = amp_full + resid_term / denominator
    return result.reshape(VIRT, VIRT, OCC * OCC)
```

```python
import functools

import jax
import jax.numpy as jnp
import numpy as np
from jax import lax
from jax.experimental import pallas as pl
from jax.experimental.pallas import tpu as pltpu
from jax.sharding import PartitionSpec as P

OCC = 16
PAIRS = OCC * OCC
BA = 32
BB = 64
LANES = 128
F32, BF16 = jnp.float32, jnp.bfloat16
MESH = pl.DeviceIdType.MESH
VMEM = pl.BlockSpec(memory_space=pltpu.VMEM)
ANY = pl.BlockSpec(memory_space=pl.ANY)
TILES = [(i, jj) for i in range(OCC) for jj in range((i + 1) // 2, OCC // 2)]
NT = len(TILES)


def spread_matrix():
    sel = np.zeros((2, NT, OCC, OCC), np.float32)
    for t, (i, jj) in enumerate(TILES):
        for jp in range(2):
            j = 2 * jj + jp
            if j > i:
                sel[jp, t, i, j] = 1.0
                sel[jp, t, j, i] = -1.0
    sel = sel.reshape(2 * NT, PAIRS)
    return np.concatenate([sel, sel], 0)


def trade_chunks(blocks):
    lane = lax.broadcasted_iota(jnp.int32, blocks[0].shape, 1)
    blocks = list(blocks)
    for d in (4, 2, 1):
        upper = (lane & (16 * d)) != 0
        for c in range(8):
            if c & d:
                continue
            lo, hi = blocks[c], blocks[c + d]
            blocks[c] = jnp.where(upper, pltpu.roll(hi, 16 * d, 1), lo)
            blocks[c + d] = jnp.where(upper, hi, pltpu.roll(lo, LANES - 16 * d, 1))
    return blocks


def arrange_kernel(a_ref, w_ref, at_ref, wt_ref, wide0, wide1):
    wides = (wide0, wide1)
    for h, wide in enumerate(wides):
        wide[...] = a_ref[:, :, h * LANES:(h + 1) * LANES].astype(F32).reshape(BA * BB, LANES)

    def amp(g, _):
        for h, wide in enumerate(wides):
            blocks = [wide[pl.ds(g * 8 + c8, BA, stride=BB), :] for c8 in range(8)]
            for i8, out in enumerate(trade_chunks(blocks)):
                at_ref[lax.rem(g, 4), g // 4, pl.ds((h * 8 + i8) * BA, BA), :] = out.astype(BF16)
        return 0

    lax.fori_loop(0, 8, amp, 0)
    q = lax.broadcasted_iota(jnp.int32, (PAIRS, PAIRS), 0)
    r = lax.broadcasted_iota(jnp.int32, (PAIRS, PAIRS), 1)
    perm = jnp.where(((q >> 4) == (r & 15)) & ((q & 15) == (r >> 4)), 1.0, 0.0).astype(BF16)

    def integ(g, _):
        x = w_ref[pl.ds(g * 8, 8)].reshape(8 * BB, PAIRS)
        y = jnp.dot(x, perm, preferred_element_type=F32)
        for h in range(2):
            for s in range(2):
                blocks = [y[c8 * BB + s * 32:c8 * BB + s * 32 + 32, h * LANES:(h + 1) * LANES] for c8 in range(8)]
                for j8, out in enumerate(trade_chunks(blocks)):
                    wt_ref[g, pl.ds((h * 8 + j8) * BB + s * 32, 32), :] = out.astype(BF16)
        return 0

    lax.fori_loop(0, 4, integ, 0)


def cycle_kernel(at, wt, r_ref, abuf, wbuf, cbuf, dsend, drecv, dsum, xf, xb, ybuf, yf,
                 x_ss, x_rs, g_ss, g_rs, f_ss, f_rs, s_ss, s_rs, sf_ss, sf_rs, d_ss, d_rs, m_ss, m_rs, l_sem):
    row, col = lax.axis_index("row"), lax.axis_index("col")
    z, xh, k = row // 4, lax.rem(row // 2, 2), lax.rem(row, 2)
    y, xl = col // 2, lax.rem(col, 2)
    x = xh * 2 + xl

    def at4(v, s):
        return lax.rem(v + (s + 4), 4)

    def dev(x, y, z, k):
        return (z * 4 + (x // 2) * 2 + k, y * 2 + lax.rem(x, 2))

    x_dev = [dev(at4(x, r), y, z, k) for r in range(4)]
    y_dev = [dev(x, at4(y, 1), z, k), dev(x, at4(y, -1), z, k)]
    z_dev = [dev(x, y, at4(z, 1), k), dev(x, y, at4(z, -1), k)]
    sib = dev(x, y, z, 1 - k)
    turned = xl * 2 + xh
    m_dev = [dev(turned, z, y, k), dev(turned, z, y, 1 - k)]
    own_turned = jnp.logical_and(y == z, xh == xl)

    bar = pltpu.get_barrier_semaphore()
    for d in x_dev[1:] + y_dev + z_dev + [sib, m_dev[1]]:
        pl.semaphore_signal(bar, inc=1, device_id=d, device_id_type=MESH)

    @pl.when(jnp.logical_not(own_turned))
    def _():
        pl.semaphore_signal(bar, inc=1, device_id=m_dev[0], device_id_type=MESH)
        pl.semaphore_wait(bar, 10)

    @pl.when(own_turned)
    def _():
        pl.semaphore_wait(bar, 9)

    def remote(src, dst, ss, rs, to):
        return pltpu.make_async_remote_copy(
            src_ref=src, dst_ref=dst, send_sem=ss, recv_sem=rs, device_id=to, device_id_type=MESH)

    def arrived(ref, ss, rs):
        remote(ref, ref, ss, rs, sib).wait_recv()

    sends = []

    def go(*args):
        copy = remote(*args)
        copy.start()
        sends.append(copy)

    own_a = pltpu.make_async_copy(at.at[x], abuf.at[y, x], l_sem.at[0])
    own_w = pltpu.make_async_copy(wt.at[x], wbuf.at[z, k, x], l_sem.at[1])
    own_a.start()
    own_w.start()
    for r in (1, 3, 2):
        to = at4(x, r)
        go(at.at[to], abuf.at[y, x], x_ss.at[0, r], x_rs.at[0, r], x_dev[r])
        go(wt.at[to], wbuf.at[z, k, x], x_ss.at[1, r], x_rs.at[1, r], x_dev[r])

    def ring(r):
        src = at4(x, -r)
        a_from = at.at[x] if r == 0 else abuf.at[y, src]
        w_from = wt.at[x] if r == 0 else wbuf.at[z, k, src]
        if r:
            arrived(abuf.at[y, src], x_ss.at[0, r], x_rs.at[0, r])
        for d in range(2):
            go(a_from, abuf.at[y, src], g_ss.at[0, d, r], g_rs.at[0, d, r], y_dev[d])
        if r:
            arrived(wbuf.at[z, k, src], x_ss.at[1, r], x_rs.at[1, r])
        for d in range(2):
            go(w_from, wbuf.at[z, k, src], g_ss.at[1, d, r], g_rs.at[1, d, r], z_dev[d])
        go(w_from, wbuf.at[z, k, src], s_ss.at[0, r], s_rs.at[0, r], sib)

    def forward(r):
        src = at4(x, -r)
        for d in range(2):
            yy, zz = at4(y, 2 * d - 1), at4(z, 2 * d - 1)
            arrived(abuf.at[yy, src], g_ss.at[0, d, r], g_rs.at[0, d, r])
            go(abuf.at[yy, src, d], abuf.at[yy, src, d], f_ss.at[0, d, r], f_rs.at[0, d, r], y_dev[d])
            arrived(wbuf.at[zz, k, src], g_ss.at[1, d, r], g_rs.at[1, d, r])
            half = wbuf.at[zz, k, src, pl.ds(d * 512, 512)]
            go(half, half, f_ss.at[1, d, r], f_rs.at[1, d, r], z_dev[d])
            go(wbuf.at[zz, k, src], wbuf.at[zz, k, src], s_ss.at[1 + d, r], s_rs.at[1 + d, r], sib)

    def finish(r):
        src = at4(x, -r)
        yy, zz = at4(y, 2), at4(z, 2)
        for d in range(2):
            arrived(abuf.at[yy, src, d], f_ss.at[0, d, r], f_rs.at[0, d, r])
            half = wbuf.at[zz, k, src, pl.ds(d * 512, 512)]
            arrived(half, f_ss.at[1, d, r], f_rs.at[1, d, r])
            go(half, half, sf_ss.at[d, r], sf_rs.at[d, r], sib)

    ring(0)
    forward(0)
    ring(1)
    ring(3)
    finish(0)
    forward(1)
    ring(2)
    forward(3)
    finish(1)
    forward(2)
    finish(3)
    finish(2)
    own_a.wait()
    own_w.wait()
    for r in range(4):
        src = at4(x, -r)
        arrived(wbuf.at[z, 1 - k, src], s_ss.at[0, r], s_rs.at[0, r])
        for d in range(2):
            zz = at4(z, 2 * d - 1)
            arrived(wbuf.at[zz, 1 - k, src], s_ss.at[1 + d, r], s_rs.at[1 + d, r])
            arrived(wbuf.at[at4(z, 2), 1 - k, src, pl.ds(d * 512, 512)], sf_ss.at[d, r], sf_rs.at[d, r])

    lane = lax.broadcasted_iota(jnp.int32, (BA, LANES), 1)
    left = lane < BB

    def quadrant(s, _):
        to = lax.rem(x + s + 1, 4)
        th, tl = to // 2, lax.rem(to, 2)
        split = [(hi, mid, lo) for hi in range(4) for mid in range(2) for lo in range(2)]

        def columns(n, _):
            lhs = jnp.concatenate([abuf[hi, 2 * th + mid, lo] for hi, mid, lo in split], axis=1)
            rhs = jnp.concatenate([wbuf[hi, lo, 2 * mid + tl, pl.ds(n * 256, 256)] for hi, mid, lo in split], axis=1)
            cbuf[:, pl.ds(pl.multiple_of(n * 256, 256), 256)] = lax.dot_general(
                lhs, rhs, (((1,), (1,)), ((), ())), preferred_element_type=F32)
            return 0

        lax.fori_loop(0, 4, columns, 0)
        for t, (i, jj) in enumerate(TILES):
            ii, ip = i // 2, i % 2
            here = cbuf[i * BA:(i + 1) * BA, jj * LANES:(jj + 1) * LANES]
            even = cbuf[2 * jj * BA:(2 * jj + 1) * BA, ii * LANES:(ii + 1) * LANES]
            odd = cbuf[(2 * jj + 1) * BA:(2 * jj + 2) * BA, ii * LANES:(ii + 1) * LANES]
            if ip == 0:
                other = jnp.where(left, even, pltpu.roll(odd, BB, 1))
            else:
                other = jnp.where(left, pltpu.roll(even, BB, 1), odd)
            tile = here - other
            dsum[t * BA:(t + 1) * BA, :] = tile
            dsend[s, t * BA:(t + 1) * BA, :] = tile.astype(BF16)

        @pl.when(s < 3)
        def _():
            remote(dsend.at[s], drecv.at[s], d_ss.at[s], d_rs.at[s], dev(to, y, z, k)).start()
        return 0

    lax.fori_loop(0, 4, quadrant, 0)
    for s in range(3):
        arrived(drecv.at[s], d_ss.at[s], d_rs.at[s])
    dsum[...] = dsum[...] + drecv[0].astype(F32) + drecv[1].astype(F32) + drecv[2].astype(F32)

    left2 = lax.broadcasted_iota(jnp.int32, (BB, LANES), 1) < BB

    def turn(p, _):
        rows = jnp.concatenate([dsum[pl.ds(2 * p + q, NT, stride=BA), :] for q in range(2)], axis=0)
        t = rows.T
        lo, hi = t[:BB], t[BB:]
        first = jnp.where(left2, lo, pltpu.roll(hi, BB, 1))
        second = jnp.where(left2, pltpu.roll(lo, BB, 1), hi)
        xf[2 * p] = first
        xf[2 * p + 1] = second
        xb[2 * p] = first.astype(BF16)
        xb[2 * p + 1] = second.astype(BF16)
        return 0

    lax.fori_loop(0, BA // 2, turn, 0)
    mine = xb.at[:, pl.ds(pl.multiple_of(k * BA, BA), BA)]
    other = xb.at[:, pl.ds(pl.multiple_of((1 - k) * BA, BA), BA)]
    go(other, ybuf.at[k], m_ss.at[1], m_rs.at[1], m_dev[1])

    @pl.when(own_turned)
    def _():
        copy = pltpu.make_async_copy(mine, ybuf.at[k], l_sem.at[2])
        copy.start()
        copy.wait()

    @pl.when(jnp.logical_not(own_turned))
    def _():
        copy = remote(mine, ybuf.at[k], m_ss.at[0], m_rs.at[0], m_dev[0])
        copy.start()
        copy.wait()

    arrived(ybuf.at[1 - k], m_ss.at[1], m_rs.at[1])
    yf[...] = ybuf[...].astype(F32).reshape(2 * BA * BA, LANES)

    def mirror(a, _):
        r_ref[a] = xf[a] - yf[pl.ds(a, BB, stride=BA), :]
        return 0

    lax.fori_loop(0, BA, mirror, 0)
    for copy in sends:
        copy.wait_send()
    for s in range(3):
        remote(dsend.at[s], drecv.at[s], d_ss.at[s], d_rs.at[s], sib).wait_send()


STEP = 8


def update_kernel(a_ref, r_ref, sel_ref, occ_ref, vrow_ref, vcol_ref, o_ref):
    r = r_ref[...].reshape(STEP * BB, LANES)
    hi = r.astype(BF16)
    lo = (r - hi.astype(F32)).astype(BF16)
    full = jnp.dot(jnp.concatenate([hi, lo], axis=1), sel_ref[...], preferred_element_type=F32)
    den = (occ_ref[...][None] - vrow_ref[...]) - vcol_ref[...][None]
    o_ref[...] = a_ref[...].astype(F32) + full.reshape(STEP, BB, PAIRS) / den


def local(amplitudes, integrals, occ_energy, vir_energy):
    at, wt = pl.pallas_call(
        arrange_kernel,
        out_shape=(jax.ShapeDtypeStruct((4, 2, 512, LANES), BF16), jax.ShapeDtypeStruct((4, 1024, LANES), BF16)),
        in_specs=[VMEM, VMEM],
        out_specs=(VMEM, VMEM),
        scratch_shapes=[pltpu.VMEM((BA * BB, LANES), F32)] * 2,
        compiler_params=pltpu.CompilerParams(vmem_limit_bytes=40 << 20),
        name="arrange",
    )(amplitudes, integrals)
    dma = pltpu.SemaphoreType.DMA
    resid = pl.pallas_call(
        cycle_kernel,
        out_shape=jax.ShapeDtypeStruct((BA, BB, LANES), F32),
        in_specs=[ANY, ANY],
        out_specs=VMEM,
        scratch_shapes=[
            pltpu.VMEM((4, 4, 2, 512, LANES), BF16),
            pltpu.VMEM((4, 2, 4, 1024, LANES), BF16),
            pltpu.VMEM((512, 1024), F32),
            pltpu.VMEM((4, NT * BA, LANES), BF16),
            pltpu.VMEM((3, NT * BA, LANES), BF16),
            pltpu.VMEM((NT * BA, LANES), F32),
            pltpu.VMEM((BA, BB, LANES), F32),
            pltpu.VMEM((BA, BB, LANES), BF16),
            pltpu.VMEM((2, BA, BA, LANES), BF16),
            pltpu.VMEM((2 * BA * BA, LANES), F32),
            dma((2, 4)), dma((2, 4)), dma((2, 2, 4)), dma((2, 2, 4)), dma((2, 2, 4)), dma((2, 2, 4)),
            dma((3, 4)), dma((3, 4)), dma((2, 4)), dma((2, 4)), dma((3,)), dma((3,)), dma((2,)), dma((2,)), dma((3,)),
        ],
        compiler_params=pltpu.CompilerParams(collective_id=0, has_side_effects=True, vmem_limit_bytes=48 << 20),
        name="cycle",
    )(at, wt)
    row_pos, col_pos = lax.axis_index("row"), lax.axis_index("col")
    vir_rows = lax.dynamic_slice_in_dim(vir_energy, row_pos * BA, BA).reshape(BA, 1, 1)
    vir_cols = lax.dynamic_slice_in_dim(vir_energy, col_pos * BB, BB).reshape(BB, 1)
    occ = (occ_energy[:, None] + occ_energy[None, :]).reshape(1, PAIRS)
    sel = jnp.asarray(spread_matrix(), BF16)
    return pl.pallas_call(
        update_kernel,
        grid=(BA // STEP,),
        out_shape=jax.ShapeDtypeStruct((BA, BB, PAIRS), F32),
        in_specs=[
            pl.BlockSpec((STEP, BB, PAIRS), lambda s: (s, 0, 0)),
            pl.BlockSpec((STEP, BB, LANES), lambda s: (s, 0, 0)),
            pl.BlockSpec((2 * LANES, PAIRS), lambda s: (0, 0)),
            pl.BlockSpec((1, PAIRS), lambda s: (0, 0)),
            pl.BlockSpec((STEP, 1, 1), lambda s: (s, 0, 0)),
            pl.BlockSpec((BB, 1), lambda s: (0, 0)),
        ],
        out_specs=pl.BlockSpec((STEP, BB, PAIRS), lambda s: (s, 0, 0)),
        compiler_params=pltpu.CompilerParams(vmem_limit_bytes=40 << 20),
        name="update",
    )(amplitudes, resid, sel, occ, vir_rows, vir_cols)


def solution(mesh):
    placed = (P("row", "col", None), P("row", "col", None), P(), P())
    return jax.shard_map(
        local, mesh=mesh, in_specs=placed, out_specs=P("row", "col", None), check_vma=False
    )
```

```python
import functools

import jax
import jax.numpy as jnp
import numpy as np
from jax import lax
from jax.experimental import pallas as pl
from jax.experimental.pallas import tpu as pltpu
from jax.sharding import PartitionSpec as P

OCC = 16
PAIRS = OCC * OCC
BA = 32
BB = 64
LANES = 128
F32, BF16 = jnp.float32, jnp.bfloat16
MESH = pl.DeviceIdType.MESH
VMEM = pl.BlockSpec(memory_space=pltpu.VMEM)
ANY = pl.BlockSpec(memory_space=pl.ANY)
TILES = [(i, jj) for i in range(OCC) for jj in range((i + 1) // 2, OCC // 2)]
NT = len(TILES)


def spread_matrix():
    sel = np.zeros((2, NT, OCC, OCC), np.float32)
    for t, (i, jj) in enumerate(TILES):
        for jp in range(2):
            j = 2 * jj + jp
            if j > i:
                sel[jp, t, i, j] = 1.0
                sel[jp, t, j, i] = -1.0
    sel = sel.reshape(2 * NT, PAIRS)
    return np.concatenate([sel, sel], 0)


def trade_chunks(blocks):
    lane = lax.broadcasted_iota(jnp.int32, blocks[0].shape, 1)
    blocks = list(blocks)
    for d in (4, 2, 1):
        upper = (lane & (16 * d)) != 0
        for c in range(8):
            if c & d:
                continue
            lo, hi = blocks[c], blocks[c + d]
            blocks[c] = jnp.where(upper, pltpu.roll(hi, 16 * d, 1), lo)
            blocks[c + d] = jnp.where(upper, hi, pltpu.roll(lo, LANES - 16 * d, 1))
    return blocks


def cycle_kernel(a_hbm, w_hbm, r_ref, av, wv, wide0, wide1, atb, wtb, abuf, wbuf, cbuf, dsend, drecv, dsum, xf, xb, ybuf, yf,
                 x_ss, x_rs, g_ss, g_rs, f_ss, f_rs, s_ss, s_rs, sf_ss, sf_rs, d_ss, d_rs, m_ss, m_rs, l_sem):
    row, col = lax.axis_index("row"), lax.axis_index("col")
    z, xh, k = row // 4, lax.rem(row // 2, 2), lax.rem(row, 2)
    y, xl = col // 2, lax.rem(col, 2)
    x = xh * 2 + xl

    def at4(v, s):
        return lax.rem(v + (s + 4), 4)

    def dev(x, y, z, k):
        return (z * 4 + (x // 2) * 2 + k, y * 2 + lax.rem(x, 2))

    x_dev = [dev(at4(x, r), y, z, k) for r in range(4)]
    y_dev = [dev(x, at4(y, 1), z, k), dev(x, at4(y, -1), z, k)]
    z_dev = [dev(x, y, at4(z, 1), k), dev(x, y, at4(z, -1), k)]
    sib = dev(x, y, z, 1 - k)
    turned = xl * 2 + xh
    m_dev = [dev(turned, z, y, k), dev(turned, z, y, 1 - k)]
    own_turned = jnp.logical_and(y == z, xh == xl)

    bar = pltpu.get_barrier_semaphore()
    for d in x_dev[1:] + y_dev + z_dev + [sib, m_dev[1]]:
        pl.semaphore_signal(bar, inc=1, device_id=d, device_id_type=MESH)

    @pl.when(jnp.logical_not(own_turned))
    def _():
        pl.semaphore_signal(bar, inc=1, device_id=m_dev[0], device_id_type=MESH)

    load_a = pltpu.make_async_copy(a_hbm, av, l_sem.at[0])
    load_w = pltpu.make_async_copy(w_hbm, wv, l_sem.at[1])
    load_w.start()
    load_a.start()

    def remote(src, dst, ss, rs, to):
        return pltpu.make_async_remote_copy(
            src_ref=src, dst_ref=dst, send_sem=ss, recv_sem=rs, device_id=to, device_id_type=MESH)

    def arrived(ref, ss, rs):
        remote(ref, ref, ss, rs, sib).wait_recv()

    sends = []

    def go(*args):
        copy = remote(*args)
        copy.start()
        sends.append(copy)

    q = lax.broadcasted_iota(jnp.int32, (PAIRS, PAIRS), 0)
    r = lax.broadcasted_iota(jnp.int32, (PAIRS, PAIRS), 1)
    perm = jnp.where(((q >> 4) == (r & 15)) & ((q & 15) == (r >> 4)), 1.0, 0.0).astype(BF16)

    def arrange_w(share, out):
        wp = jnp.dot(wv[pl.ds(share * 8, 8)].reshape(8 * BB, PAIRS), perm, preferred_element_type=F32)
        for h in range(2):
            for s in range(2):
                blocks = [wp[c8 * BB + s * 32:c8 * BB + s * 32 + 32, h * LANES:(h + 1) * LANES] for c8 in range(8)]
                for j8, v in enumerate(trade_chunks(blocks)):
                    at = (h * 8 + j8) * BB + s * 32
                    out[at:at + 32, :] = v.astype(BF16)

    def arrange_a(share, out):
        for lo in range(2):
            for h, wide in enumerate((wide0, wide1)):
                blocks = [wide[pl.ds((share + 4 * lo) * 8 + c8, BA, stride=BB), :] for c8 in range(8)]
                for i8, v in enumerate(trade_chunks(blocks)):
                    at = (h * 8 + i8) * 16
                    v = v.astype(BF16)
                    out[lo, at:at + 16, :] = v[:16]
                    out[lo, 256 + at:256 + at + 16, :] = v[16:]

    load_w.wait()
    arrange_w(x, wbuf.at[z, k, x])

    @pl.when(own_turned)
    def _():
        pl.semaphore_wait(bar, 9)

    @pl.when(jnp.logical_not(own_turned))
    def _():
        pl.semaphore_wait(bar, 10)

    def ring_w(r):
        src = at4(x, -r)
        if r:
            arrived(wbuf.at[z, k, src], x_ss.at[1, r], x_rs.at[1, r])
        for d in range(2):
            go(wbuf.at[z, k, src], wbuf.at[z, k, src], g_ss.at[1, d, r], g_rs.at[1, d, r], z_dev[d])
        go(wbuf.at[z, k, src], wbuf.at[z, k, src], s_ss.at[0, r], s_rs.at[0, r], sib)

    def ring_a(r):
        src = at4(x, -r)
        if r:
            arrived(abuf.at[y, src], x_ss.at[0, r], x_rs.at[0, r])
        for d in range(2):
            go(abuf.at[y, src], abuf.at[y, src], g_ss.at[0, d, r], g_rs.at[0, d, r], y_dev[d])

    ring_w(0)
    load_a.wait()
    for h, wide in enumerate((wide0, wide1)):
        wide[...] = av[:, :, h * LANES:(h + 1) * LANES].astype(F32).reshape(BA * BB, LANES)
    arrange_a(x, abuf.at[y, x])
    ring_a(0)

    def share_out(n, _):
        r = (1 + 2 * n) - 3 * (n // 2)
        to = at4(x, r)
        there = dev(to, y, z, k)
        arrange_w(to, wtb.at[n])
        remote(wtb.at[n], wbuf.at[z, k, x], x_ss.at[1, r], x_rs.at[1, r], there).start()
        arrange_a(to, atb.at[n])
        remote(atb.at[n], abuf.at[y, x], x_ss.at[0, r], x_rs.at[0, r], there).start()
        return 0

    lax.fori_loop(0, 3, share_out, 0)

    def forward(r):
        src = at4(x, -r)
        for d in range(2):
            yy, zz = at4(y, 2 * d - 1), at4(z, 2 * d - 1)
            arrived(wbuf.at[zz, k, src], g_ss.at[1, d, r], g_rs.at[1, d, r])
            half = wbuf.at[zz, k, src, pl.ds(d * 512, 512)]
            go(half, half, f_ss.at[1, d, r], f_rs.at[1, d, r], z_dev[d])
            go(wbuf.at[zz, k, src], wbuf.at[zz, k, src], s_ss.at[1 + d, r], s_rs.at[1 + d, r], sib)
            arrived(abuf.at[yy, src], g_ss.at[0, d, r], g_rs.at[0, d, r])
            go(abuf.at[yy, src, d], abuf.at[yy, src, d], f_ss.at[0, d, r], f_rs.at[0, d, r], y_dev[d])

    def finish(r):
        src = at4(x, -r)
        yy, zz = at4(y, 2), at4(z, 2)
        for d in range(2):
            half = wbuf.at[zz, k, src, pl.ds(d * 512, 512)]
            arrived(half, f_ss.at[1, d, r], f_rs.at[1, d, r])
            go(half, half, sf_ss.at[d, r], sf_rs.at[d, r], sib)
            arrived(abuf.at[yy, src, d], f_ss.at[0, d, r], f_rs.at[0, d, r])

    forward(0)
    ring_w(1)
    ring_a(1)
    ring_w(3)
    ring_a(3)
    finish(0)
    forward(1)
    ring_w(2)
    ring_a(2)
    forward(3)
    finish(1)
    forward(2)
    finish(3)
    finish(2)
    for r in range(4):
        src = at4(x, -r)
        arrived(wbuf.at[z, 1 - k, src], s_ss.at[0, r], s_rs.at[0, r])
        for d in range(2):
            zz = at4(z, 2 * d - 1)
            arrived(wbuf.at[zz, 1 - k, src], s_ss.at[1 + d, r], s_rs.at[1 + d, r])
            arrived(wbuf.at[at4(z, 2), 1 - k, src, pl.ds(d * 512, 512)], sf_ss.at[d, r], sf_rs.at[d, r])

    left = lax.broadcasted_iota(jnp.int32, (16, LANES), 1) < BB

    def quadrant(n, _):
        h, s = n // 4, lax.rem(n, 4)
        to = lax.rem(x + s + 1, 4)
        th, tl = to // 2, lax.rem(to, 2)
        split = [(hi, mid, lo) for hi in range(4) for mid in range(2) for lo in range(2)]

        def columns(n, _):
            rows = pl.ds(pl.multiple_of(h * 256, 256), 256)
            lhs = jnp.concatenate([abuf[hi, 2 * th + mid, lo, rows] for hi, mid, lo in split], axis=1)
            rhs = jnp.concatenate([wbuf[hi, lo, 2 * mid + tl, pl.ds(n * 512, 512)] for hi, mid, lo in split], axis=1)
            cbuf[:, pl.ds(pl.multiple_of(n * 512, 512), 512)] = lax.dot_general(
                lhs, rhs, (((1,), (1,)), ((), ())), preferred_element_type=F32)
            return 0

        lax.fori_loop(0, 2, columns, 0)
        for t, (i, jj) in enumerate(TILES):
            ii, ip = i // 2, i % 2
            here = cbuf[i * 16:(i + 1) * 16, jj * LANES:(jj + 1) * LANES]
            even = cbuf[2 * jj * 16:(2 * jj + 1) * 16, ii * LANES:(ii + 1) * LANES]
            odd = cbuf[(2 * jj + 1) * 16:(2 * jj + 2) * 16, ii * LANES:(ii + 1) * LANES]
            if ip == 0:
                other = jnp.where(left, even, pltpu.roll(odd, BB, 1))
            else:
                other = jnp.where(left, pltpu.roll(even, BB, 1), odd)
            tile = here - other
            dsum[pl.ds(h * (NT * 16) + t * 16, 16), :] = tile
            dsend[n, t * 16:(t + 1) * 16, :] = tile.astype(BF16)

        @pl.when(s < 3)
        def _():
            remote(dsend.at[n], drecv.at[n], d_ss.at[n], d_rs.at[n], dev(to, y, z, k)).start()
        return 0

    lax.fori_loop(0, 8, quadrant, 0)

    left2 = lax.broadcasted_iota(jnp.int32, (BB, LANES), 1) < BB
    b_mine = pl.ds(pl.multiple_of(k * BA, BA), BA)
    b_other = pl.ds(pl.multiple_of((1 - k) * BA, BA), BA)
    for h in range(2):
        for s in range(3):
            arrived(drecv.at[4 * h + s], d_ss.at[4 * h + s], d_rs.at[4 * h + s])
        part = pl.ds(h * NT * 16, NT * 16)
        dsum[part, :] = (dsum[part, :] + drecv[4 * h].astype(F32) + drecv[4 * h + 1].astype(F32)
                         + drecv[4 * h + 2].astype(F32))

        def turn(p, _):
            rows = jnp.concatenate(
                [dsum[pl.ds(h * NT * 16 + 2 * p + q, NT, stride=16), :] for q in range(2)], axis=0)
            t = rows.T
            lo, hi = t[:BB], t[BB:]
            first = jnp.where(left2, lo, pltpu.roll(hi, BB, 1))
            second = jnp.where(left2, pltpu.roll(lo, BB, 1), hi)
            at = h * 16 + 2 * p
            xf[at] = first
            xf[at + 1] = second
            xb[at] = first.astype(BF16)
            xb[at + 1] = second.astype(BF16)
            return 0

        lax.fori_loop(0, 8, turn, 0)
        a_part = pl.ds(h * 16, 16)
        go(xb.at[a_part, b_other], ybuf.at[k, a_part], m_ss.at[1, h], m_rs.at[1, h], m_dev[1])
        same = (xb.at[a_part, b_mine], ybuf.at[k, a_part])

        @pl.when(own_turned)
        def _():
            pltpu.make_async_copy(*same, l_sem.at[2 + h]).start()

        @pl.when(jnp.logical_not(own_turned))
        def _():
            remote(*same, m_ss.at[0, h], m_rs.at[0, h], m_dev[0]).start()

    for h in range(2):
        a_part = pl.ds(h * 16, 16)
        same = (xb.at[a_part, b_mine], ybuf.at[k, a_part])

        @pl.when(own_turned)
        def _():
            pltpu.make_async_copy(*same, l_sem.at[2 + h]).wait()

        @pl.when(jnp.logical_not(own_turned))
        def _():
            remote(*same, m_ss.at[0, h], m_rs.at[0, h], m_dev[0]).wait()

        arrived(ybuf.at[1 - k, a_part], m_ss.at[1, h], m_rs.at[1, h])
        for c in range(2):
            at = c * BA * BA + h * 16 * BA
            yf[at:at + 16 * BA, :] = ybuf[c, h * 16:h * 16 + 16].astype(F32).reshape(16 * BA, LANES)

    def mirror(a, _):
        r_ref[a] = xf[a] - yf[pl.ds(a, BB, stride=BA), :]
        return 0

    lax.fori_loop(0, BA, mirror, 0)
    for copy in sends:
        copy.wait_send()
    for n, r in enumerate((1, 3, 2)):
        remote(wtb.at[n], wbuf.at[z, k, x], x_ss.at[1, r], x_rs.at[1, r], sib).wait_send()
        remote(atb.at[n], abuf.at[y, x], x_ss.at[0, r], x_rs.at[0, r], sib).wait_send()
    for h in range(2):
        for s in range(3):
            n = 4 * h + s
            remote(dsend.at[n], drecv.at[n], d_ss.at[n], d_rs.at[n], sib).wait_send()


STEP = 8


def update_kernel(a_ref, r_ref, sel_ref, occ_ref, vrow_ref, vcol_ref, o_ref):
    r = r_ref[...].reshape(STEP * BB, LANES)
    hi = r.astype(BF16)
    lo = (r - hi.astype(F32)).astype(BF16)
    full = jnp.dot(jnp.concatenate([hi, lo], axis=1), sel_ref[...], preferred_element_type=F32)
    den = (occ_ref[...][None] - vrow_ref[...]) - vcol_ref[...][None]
    o_ref[...] = a_ref[...].astype(F32) + full.reshape(STEP, BB, PAIRS) / den


def local(amplitudes, integrals, occ_energy, vir_energy):
    dma = pltpu.SemaphoreType.DMA
    resid = pl.pallas_call(
        cycle_kernel,
        out_shape=jax.ShapeDtypeStruct((BA, BB, LANES), F32),
        in_specs=[ANY, ANY],
        out_specs=VMEM,
        scratch_shapes=[
            pltpu.VMEM((BA, BB, PAIRS), BF16),
            pltpu.VMEM((BA, BB, PAIRS), BF16),
            pltpu.VMEM((BA * BB, LANES), F32),
            pltpu.VMEM((BA * BB, LANES), F32),
            pltpu.VMEM((3, 2, 512, LANES), BF16),
            pltpu.VMEM((3, 1024, LANES), BF16),
            pltpu.VMEM((4, 4, 2, 512, LANES), BF16),
            pltpu.VMEM((4, 2, 4, 1024, LANES), BF16),
            pltpu.VMEM((256, 1024), F32),
            pltpu.VMEM((8, NT * 16, LANES), BF16),
            pltpu.VMEM((8, NT * 16, LANES), BF16),
            pltpu.VMEM((NT * BA, LANES), F32),
            pltpu.VMEM((BA, BB, LANES), F32),
            pltpu.VMEM((BA, BB, LANES), BF16),
            pltpu.VMEM((2, BA, BA, LANES), BF16),
            pltpu.VMEM((2 * BA * BA, LANES), F32),
            dma((2, 4)), dma((2, 4)), dma((2, 2, 4)), dma((2, 2, 4)), dma((2, 2, 4)), dma((2, 2, 4)),
            dma((3, 4)), dma((3, 4)), dma((2, 4)), dma((2, 4)), dma((8,)), dma((8,)), dma((2, 2)), dma((2, 2)), dma((4,)),
        ],
        compiler_params=pltpu.CompilerParams(collective_id=0, has_side_effects=True, vmem_limit_bytes=48 << 20),
        name="cycle",
    )(amplitudes, integrals)
    row_pos, col_pos = lax.axis_index("row"), lax.axis_index("col")
    vir_rows = lax.dynamic_slice_in_dim(vir_energy, row_pos * BA, BA).reshape(BA, 1, 1)
    vir_cols = lax.dynamic_slice_in_dim(vir_energy, col_pos * BB, BB).reshape(BB, 1)
    occ = (occ_energy[:, None] + occ_energy[None, :]).reshape(1, PAIRS)
    sel = jnp.asarray(spread_matrix(), BF16)
    return pl.pallas_call(
        update_kernel,
        grid=(BA // STEP,),
        out_shape=jax.ShapeDtypeStruct((BA, BB, PAIRS), F32),
        in_specs=[
            pl.BlockSpec((STEP, BB, PAIRS), lambda s: (s, 0, 0)),
            pl.BlockSpec((STEP, BB, LANES), lambda s: (s, 0, 0)),
            pl.BlockSpec((2 * LANES, PAIRS), lambda s: (0, 0)),
            pl.BlockSpec((1, PAIRS), lambda s: (0, 0)),
            pl.BlockSpec((STEP, 1, 1), lambda s: (s, 0, 0)),
            pl.BlockSpec((BB, 1), lambda s: (0, 0)),
        ],
        out_specs=pl.BlockSpec((STEP, BB, PAIRS), lambda s: (s, 0, 0)),
        compiler_params=pltpu.CompilerParams(vmem_limit_bytes=40 << 20),
        name="update",
    )(amplitudes, resid, sel, occ, vir_rows, vir_cols)


def solution(mesh):
    placed = (P("row", "col", None), P("row", "col", None), P(), P())
    return jax.shard_map(
        local, mesh=mesh, in_specs=placed, out_specs=P("row", "col", None), check_vma=False
    )
```

```python
import functools

import jax
import jax.numpy as jnp
import numpy as np
from jax import lax
from jax.experimental import pallas as pl
from jax.experimental.pallas import tpu as pltpu
from jax.sharding import PartitionSpec as P

OCC = 16
PAIRS = OCC * OCC
BA = 32
BB = 64
LANES = 128
F32, BF16 = jnp.float32, jnp.bfloat16
MESH = pl.DeviceIdType.MESH
VMEM = pl.BlockSpec(memory_space=pltpu.VMEM)
ANY = pl.BlockSpec(memory_space=pl.ANY)
TILES = [(i, jj) for i in range(OCC) for jj in range((i + 1) // 2, OCC // 2)]
NT = len(TILES)
ROWS = NT * 8


def spread_matrix():
    sel = np.zeros((2, NT, OCC, OCC), np.float32)
    for t, (i, jj) in enumerate(TILES):
        for jp in range(2):
            j = 2 * jj + jp
            if j > i:
                sel[jp, t, i, j] = 1.0
                sel[jp, t, j, i] = -1.0
    sel = sel.reshape(2 * NT, PAIRS)
    return np.concatenate([sel, sel], 0)


def trade_chunks(blocks):
    lane = lax.broadcasted_iota(jnp.int32, blocks[0].shape, 1)
    blocks = list(blocks)
    for d in (4, 2, 1):
        upper = (lane & (16 * d)) != 0
        for c in range(8):
            if c & d:
                continue
            lo, hi = blocks[c], blocks[c + d]
            blocks[c] = jnp.where(upper, pltpu.roll(hi, 16 * d, 1), lo)
            blocks[c + d] = jnp.where(upper, hi, pltpu.roll(lo, LANES - 16 * d, 1))
    return blocks


def cycle_kernel(a_hbm, w_hbm, r_ref, av, wv, wide0, wide1, atb, wtb, ra, rw, rd, abuf, wbuf, cbuf, dsend, drecv, dsum, xf, xb, mid, ybuf, yf,
                 x_ss, x_rs, xf_ss, xf_rs, g_ss, g_rs, f_ss, f_rs, s_ss, s_rs, sf_ss, sf_rs, d_ss, d_rs, e_ss, e_rs, p_ss, m_ss, m_rs, l_sem):
    row, col = lax.axis_index("row"), lax.axis_index("col")
    z, xh, k = row // 4, lax.rem(row // 2, 2), lax.rem(row, 2)
    y, xl = col // 2, lax.rem(col, 2)
    x = xh * 2 + xl

    def at4(v, s):
        return lax.rem(v + (s + 4), 4)

    def dev(x, y, z, k):
        return (z * 4 + (x // 2) * 2 + k, y * 2 + lax.rem(x, 2))

    x_dev = [dev(at4(x, r), y, z, k) for r in range(4)]
    y_dev = [dev(x, at4(y, 1), z, k), dev(x, at4(y, -1), z, k)]
    z_dev = [dev(x, y, at4(z, 1), k), dev(x, y, at4(z, -1), k)]
    sib = dev(x, y, z, 1 - k)
    turned = xl * 2 + xh
    m_dev = [dev(turned, z, y, k), dev(turned, z, y, 1 - k)]
    diagonal = y == z
    own_turned = jnp.logical_and(diagonal, xh == xl)

    bar = pltpu.get_barrier_semaphore()

    def greet(d):
        pl.semaphore_signal(bar, inc=1, device_id=d, device_id_type=MESH)

    for d in x_dev[1:] + y_dev + z_dev + [sib]:
        greet(d)

    @pl.when(diagonal)
    def _():
        greet(m_dev[1])
        for j in range(1, 4):
            for d in (dev(turned, at4(y, j), z, k), dev(turned, y, at4(z, j), 1 - k),
                      dev(x, y, at4(z, j), k), dev(x, at4(y, j), z, k)):
                greet(d)

        @pl.when(jnp.logical_not(own_turned))
        def _():
            greet(m_dev[0])

    @pl.when(jnp.logical_not(diagonal))
    def _():
        for d in (dev(turned, z, z, k), dev(turned, y, y, 1 - k), dev(x, y, y, k), dev(x, z, z, k)):
            greet(d)

    load_a = pltpu.make_async_copy(a_hbm, av, l_sem.at[0])
    load_w = pltpu.make_async_copy(w_hbm, wv, l_sem.at[1])
    load_w.start()
    load_a.start()

    def remote(src, dst, ss, rs, to):
        return pltpu.make_async_remote_copy(
            src_ref=src, dst_ref=dst, send_sem=ss, recv_sem=rs, device_id=to, device_id_type=MESH)

    def arrived(ref, ss, rs):
        remote(ref, ref, ss, rs, sib).wait_recv()

    sends = []

    def go(*args):
        copy = remote(*args)
        copy.start()
        sends.append(copy)

    q = lax.broadcasted_iota(jnp.int32, (PAIRS, PAIRS), 0)
    r = lax.broadcasted_iota(jnp.int32, (PAIRS, PAIRS), 1)
    perm = jnp.where(((q >> 4) == (r & 15)) & ((q & 15) == (r >> 4)), 1.0, 0.0).astype(BF16)

    def arrange_w(share, out):
        wp = jnp.dot(wv[pl.ds(share * 8, 8)].reshape(8 * BB, PAIRS), perm, preferred_element_type=F32)
        for h in range(2):
            for s in range(2):
                blocks = [wp[c8 * BB + s * 32:c8 * BB + s * 32 + 32, h * LANES:(h + 1) * LANES] for c8 in range(8)]
                for j8, v in enumerate(trade_chunks(blocks)):
                    at = (h * 8 + j8) * BB + s * 32
                    out[at:at + 32, :] = v.astype(BF16)

    def arrange_a(share, out):
        for lo in range(2):
            for h, wide in enumerate((wide0, wide1)):
                blocks = [wide[pl.ds((share + 4 * lo) * 8 + c8, BA, stride=BB), :] for c8 in range(8)]
                for i8, v in enumerate(trade_chunks(blocks)):
                    at = (h * 8 + i8) * 16
                    v = v.astype(BF16)
                    out[lo, at:at + 16, :] = v[:16]
                    out[lo, 256 + at:256 + at + 16, :] = v[16:]

    load_w.wait()
    arrange_w(x, wbuf.at[z, k, x])

    @pl.when(jnp.logical_not(diagonal))
    def _():
        pl.semaphore_wait(bar, 12)

    @pl.when(own_turned)
    def _():
        pl.semaphore_wait(bar, 21)

    @pl.when(jnp.logical_and(diagonal, xh != xl))
    def _():
        pl.semaphore_wait(bar, 22)

    def ring_w(r):
        src = at4(x, -r)
        if r == 2:
            for d in range(2):
                half = wbuf.at[z, k, src, pl.ds(d * 512, 512)]
                arrived(half, xf_ss.at[1, d], xf_rs.at[1, d])
        elif r:
            arrived(wbuf.at[z, k, src], x_ss.at[1, r], x_rs.at[1, r])
        for d in range(2):
            go(wbuf.at[z, k, src], wbuf.at[z, k, src], g_ss.at[1, d, r], g_rs.at[1, d, r], z_dev[d])
        go(wbuf.at[z, k, src], wbuf.at[z, k, src], s_ss.at[0, r], s_rs.at[0, r], sib)

    def ring_a(r):
        src = at4(x, -r)
        if r == 2:
            for d in range(2):
                arrived(abuf.at[y, src, d], xf_ss.at[0, d], xf_rs.at[0, d])
        elif r:
            arrived(abuf.at[y, src], x_ss.at[0, r], x_rs.at[0, r])
        for d in range(2):
            go(abuf.at[y, src], abuf.at[y, src], g_ss.at[0, d, r], g_rs.at[0, d, r], y_dev[d])

    beside = [x_dev[1], x_dev[3]]

    def near_w(n, _):
        r = 2 * n - 1
        to = at4(x, r)
        arrange_w(to, wtb.at[n])
        remote(wtb.at[n], wbuf.at[z, k, x], x_ss.at[1, r], x_rs.at[1, r], dev(to, y, z, k)).start()
        return 0

    def near_a(n, _):
        r = 2 * n - 1
        to = at4(x, r)
        arrange_a(to, atb.at[n])
        remote(atb.at[n], abuf.at[y, x], x_ss.at[0, r], x_rs.at[0, r], dev(to, y, z, k)).start()
        return 0

    def stage_w():
        for d in range(2):
            go(wtb.at[0, pl.ds(d * 512, 512)], rw.at[d], x_ss.at[1, 2 * d], x_rs.at[1, 2 * d], beside[d])

    def stage_a():
        for d in range(2):
            go(atb.at[0, d], ra.at[d], x_ss.at[0, 2 * d], x_rs.at[0, 2 * d], beside[d])

    def relay_w():
        for d in range(2):
            arrived(rw.at[d], x_ss.at[1, 2 * d], x_rs.at[1, 2 * d])
            go(rw.at[d], wbuf.at[z, k, at4(x, 2 * d - 1), pl.ds(d * 512, 512)], xf_ss.at[1, d], xf_rs.at[1, d], beside[d])

    def relay_a():
        for d in range(2):
            arrived(ra.at[d], x_ss.at[0, 2 * d], x_rs.at[0, 2 * d])
            go(ra.at[d], abuf.at[y, at4(x, 2 * d - 1), d], xf_ss.at[0, d], xf_rs.at[0, d], beside[d])

    def forward_w(r):
        src = at4(x, -r)
        for d in range(2):
            zz = at4(z, 2 * d - 1)
            arrived(wbuf.at[zz, k, src], g_ss.at[1, d, r], g_rs.at[1, d, r])
            half = wbuf.at[zz, k, src, pl.ds(d * 512, 512)]
            go(half, half, f_ss.at[1, d, r], f_rs.at[1, d, r], z_dev[d])
            go(wbuf.at[zz, k, src], wbuf.at[zz, k, src], s_ss.at[1 + d, r], s_rs.at[1 + d, r], sib)

    def forward_a(r):
        src = at4(x, -r)
        for d in range(2):
            yy = at4(y, 2 * d - 1)
            arrived(abuf.at[yy, src], g_ss.at[0, d, r], g_rs.at[0, d, r])
            go(abuf.at[yy, src, d], abuf.at[yy, src, d], f_ss.at[0, d, r], f_rs.at[0, d, r], y_dev[d])

    def finish_w(r):
        for d in range(2):
            half = wbuf.at[at4(z, 2), k, at4(x, -r), pl.ds(d * 512, 512)]
            arrived(half, f_ss.at[1, d, r], f_rs.at[1, d, r])
            go(half, half, sf_ss.at[d, r], sf_rs.at[d, r], sib)

    def finish_a(r):
        for d in range(2):
            arrived(abuf.at[at4(y, 2), at4(x, -r), d], f_ss.at[0, d, r], f_rs.at[0, d, r])

    ring_w(0)
    lax.fori_loop(1, 3, near_w, 0)
    load_a.wait()
    for h, wide in enumerate((wide0, wide1)):
        wide[...] = av[:, :, h * LANES:(h + 1) * LANES].astype(F32).reshape(BA * BB, LANES)
    arrange_a(x, abuf.at[y, x])
    ring_a(0)
    lax.fori_loop(1, 3, near_a, 0)
    arrange_w(at4(x, 2), wtb.at[0])
    arrange_a(at4(x, 2), atb.at[0])
    forward_w(0)
    ring_w(1)
    ring_w(3)
    stage_w()
    forward_a(0)
    ring_a(1)
    ring_a(3)
    stage_a()
    forward_w(1)
    relay_w()
    forward_a(1)
    relay_a()
    ring_w(2)
    forward_w(3)
    ring_a(2)
    forward_a(3)
    finish_w(0)
    finish_w(1)
    forward_w(2)
    finish_w(3)
    forward_a(2)
    finish_w(2)
    for r in (0, 1, 3, 2):
        finish_a(r)
    for r in range(4):
        src = at4(x, -r)
        arrived(wbuf.at[z, 1 - k, src], s_ss.at[0, r], s_rs.at[0, r])
        for d in range(2):
            zz = at4(z, 2 * d - 1)
            arrived(wbuf.at[zz, 1 - k, src], s_ss.at[1 + d, r], s_rs.at[1 + d, r])
            arrived(wbuf.at[at4(z, 2), 1 - k, src, pl.ds(d * 512, 512)], sf_ss.at[d, r], sf_rs.at[d, r])

    left = lax.broadcasted_iota(jnp.int32, (16, LANES), 1) < BB

    def quadrant(n, _):
        h, s = n // 4, lax.rem(n, 4)
        to = lax.rem(x + 2 - s + 3 * (s // 2) + 2 * (s // 3), 4)
        th, tl = to // 2, lax.rem(to, 2)
        split = [(hi, mid, lo) for hi in range(4) for mid in range(2) for lo in range(2)]

        def columns(n, _):
            rows = pl.ds(pl.multiple_of(h * 256, 256), 256)
            lhs = jnp.concatenate([abuf[hi, 2 * th + mid, lo, rows] for hi, mid, lo in split], axis=1)
            rhs = jnp.concatenate([wbuf[hi, lo, 2 * mid + tl, pl.ds(n * 512, 512)] for hi, mid, lo in split], axis=1)
            cbuf[:, pl.ds(pl.multiple_of(n * 512, 512), 512)] = lax.dot_general(
                lhs, rhs, (((1,), (1,)), ((), ())), preferred_element_type=F32)
            return 0

        lax.fori_loop(0, 2, columns, 0)
        tiles = []
        for t, (i, jj) in enumerate(TILES):
            ii, ip = i // 2, i % 2
            here = cbuf[i * 16:(i + 1) * 16, jj * LANES:(jj + 1) * LANES]
            even = cbuf[2 * jj * 16:(2 * jj + 1) * 16, ii * LANES:(ii + 1) * LANES]
            odd = cbuf[(2 * jj + 1) * 16:(2 * jj + 2) * 16, ii * LANES:(ii + 1) * LANES]
            if ip == 0:
                other = jnp.where(left, even, pltpu.roll(odd, BB, 1))
            else:
                other = jnp.where(left, pltpu.roll(even, BB, 1), odd)
            tiles.append(here - other)
            if t % 2 == 0:
                continue
            for u in range(2):
                pair = jnp.concatenate([v[u * 8:u * 8 + 8] for v in tiles], axis=0)
                dsum[pl.ds((2 * h + u) * ROWS + (t - 1) * 8, 16), :] = pair
                dsend[n, u, (t - 1) * 8:(t + 1) * 8, :] = pair.astype(BF16)
            tiles = []

        @pl.when(s == 0)
        def _():
            stage_d(2 * h)

        @pl.when(lax.rem(s, 3) > 0)
        def _():
            near_d(2 * h, s)

        @pl.when(s == 3)
        def _():
            relay_d(2 * h)
            stage_d(2 * h + 1)
            near_d(2 * h + 1, 1)
            near_d(2 * h + 1, 2)

        @pl.when(n == 5)
        def _():
            relay_d(1)
        return 0

    def term(c, s):
        return dsend.at[4 * (c // 2) + s, lax.rem(c, 2)]

    def d_copy(c, e, src, dst, to):
        return remote(src, dst, d_ss.at[c, e], d_rs.at[c, e], to)

    def stage_copy(c, d):
        return d_copy(c, d, term(c, 0).at[pl.ds(d * ROWS // 2, ROWS // 2)], rd.at[c, d], beside[d])

    def near_copy(c, s):
        return d_copy(c, s + 1, term(c, s), drecv.at[c, s], dev(at4(x, 3 - 2 * (2 - s)), y, z, k))

    def relay_copy(c, d):
        return d_copy(c, 4 + d, rd.at[c, d], drecv.at[c, 0, pl.ds(d * ROWS // 2, ROWS // 2)], beside[d])

    def stage_d(c):
        for d in range(2):
            stage_copy(c, d).start()

    def near_d(c, s):
        near_copy(c, s).start()

    def relay_d(c):
        for d in range(2):
            stage_copy(c, d).wait_recv()
            relay_copy(c, d).start()

    lax.fori_loop(0, 8, quadrant, 0)
    relay_d(3)

    left2 = lax.broadcasted_iota(jnp.int32, (BB, LANES), 1) < BB

    def block(q, c):
        return xb.at[(k, 1 - k)[q], pl.ds(c * 8, 8)]

    def direct(q, c):
        return remote(block(q, c), ybuf.at[k, pl.ds(c * 8, 8)], m_ss.at[q, c], m_rs.at[q, c], m_dev[q])

    def same_chip(c):
        return pltpu.make_async_copy(block(0, c), ybuf.at[k, pl.ds(c * 8, 8)], l_sem.at[2 + c])

    def to_corner(q, c):
        if q == 0:
            corner, slot = dev(turned, z, z, k), lax.rem(y - z + 3, 4)
        else:
            corner, slot = dev(turned, y, y, 1 - k), lax.rem(z - y + 3, 4)
        return remote(block(q, c), mid.at[q, c, slot], e_ss.at[q, c], e_rs.at[q, c, slot], corner)

    def from_corner(q, c, j):
        there = dev(x, y, at4(z, 1 + j), k) if q == 0 else dev(x, at4(y, 1 + j), z, k)
        slot = k if q == 0 else 1 - k
        return remote(mid.at[q, c, j], ybuf.at[slot, pl.ds(c * 8, 8)], p_ss.at[q, c, j], m_rs.at[q, c], there)

    def pass_on(c):
        @pl.when(diagonal)
        def _():
            for q in range(2):
                def one(j, _):
                    arrived(mid.at[q, c, j], e_ss.at[q, c], e_rs.at[q, c, j])
                    from_corner(q, c, j).start()
                    return 0

                lax.fori_loop(0, 3, one, 0)

    for c in range(4):
        for s in (1, 2):
            near_copy(c, s).wait_recv()
        for d in range(2):
            relay_copy(c, d).wait_recv()
        part = pl.ds(c * ROWS, ROWS)
        dsum[part, :] = dsum[part, :] + drecv[c, 0].astype(F32) + drecv[c, 1].astype(F32) + drecv[c, 2].astype(F32)

        def turn(p, _):
            rows = jnp.concatenate(
                [dsum[pl.ds(c * ROWS + 2 * p + q, NT, stride=8), :] for q in range(2)], axis=0)
            t = rows.T
            lo, hi = t[:BB], t[BB:]
            first = jnp.where(left2, lo, pltpu.roll(hi, BB, 1))
            second = jnp.where(left2, pltpu.roll(lo, BB, 1), hi)
            at = c * 8 + 2 * p
            xf[at] = first
            xf[at + 1] = second
            xb[0, at] = first[:BA].astype(BF16)
            xb[1, at] = first[BA:].astype(BF16)
            xb[0, at + 1] = second[:BA].astype(BF16)
            xb[1, at + 1] = second[BA:].astype(BF16)
            return 0

        lax.fori_loop(0, 4, turn, 0)

        @pl.when(jnp.logical_not(diagonal))
        def _():
            to_corner(0, c).start()
            to_corner(1, c).start()

        @pl.when(diagonal)
        def _():
            direct(1, c).start()

            @pl.when(own_turned)
            def _():
                same_chip(c).start()

            @pl.when(jnp.logical_not(own_turned))
            def _():
                direct(0, c).start()

        if c:
            pass_on(c - 1)
    pass_on(3)

    for c in range(4):
        @pl.when(own_turned)
        def _():
            same_chip(c).wait()

        @pl.when(jnp.logical_not(own_turned))
        def _():
            arrived(ybuf.at[k, pl.ds(c * 8, 8)], m_ss.at[0, c], m_rs.at[0, c])

        arrived(ybuf.at[1 - k, pl.ds(c * 8, 8)], m_ss.at[1, c], m_rs.at[1, c])
        for v in range(2):
            at = v * BA * BA + c * 8 * BA
            yf[at:at + 8 * BA, :] = ybuf[v, c * 8:c * 8 + 8].astype(F32).reshape(8 * BA, LANES)

    def mirror(a, _):
        r_ref[a] = xf[a] - yf[pl.ds(a, BB, stride=BA), :]
        return 0

    lax.fori_loop(0, BA, mirror, 0)
    for copy in sends:
        copy.wait_send()
    for n, r in ((1, 1), (2, 3)):
        remote(wtb.at[n], wbuf.at[z, k, x], x_ss.at[1, r], x_rs.at[1, r], sib).wait_send()
        remote(atb.at[n], abuf.at[y, x], x_ss.at[0, r], x_rs.at[0, r], sib).wait_send()
    for c in range(4):
        for s in (1, 2):
            near_copy(c, s).wait_send()
        for d in range(2):
            stage_copy(c, d).wait_send()
            relay_copy(c, d).wait_send()

        @pl.when(jnp.logical_not(diagonal))
        def _():
            to_corner(0, c).wait_send()
            to_corner(1, c).wait_send()

        @pl.when(diagonal)
        def _():
            direct(1, c).wait_send()
            for q in range(2):
                for j in range(3):
                    from_corner(q, c, j).wait_send()

            @pl.when(jnp.logical_not(own_turned))
            def _():
                direct(0, c).wait_send()


STEP = 8


def update_kernel(a_ref, r_ref, sel_ref, occ_ref, vrow_ref, vcol_ref, o_ref):
    r = r_ref[...].reshape(STEP * BB, LANES)
    hi = r.astype(BF16)
    lo = (r - hi.astype(F32)).astype(BF16)
    full = jnp.dot(jnp.concatenate([hi, lo], axis=1), sel_ref[...], preferred_element_type=F32)
    den = (occ_ref[...][None] - vrow_ref[...]) - vcol_ref[...][None]
    o_ref[...] = a_ref[...].astype(F32) + full.reshape(STEP, BB, PAIRS) / den


def local(amplitudes, integrals, occ_energy, vir_energy):
    dma = pltpu.SemaphoreType.DMA
    resid = pl.pallas_call(
        cycle_kernel,
        out_shape=jax.ShapeDtypeStruct((BA, BB, LANES), F32),
        in_specs=[ANY, ANY],
        out_specs=VMEM,
        scratch_shapes=[
            pltpu.VMEM((BA, BB, PAIRS), BF16),
            pltpu.VMEM((BA, BB, PAIRS), BF16),
            pltpu.VMEM((BA * BB, LANES), F32),
            pltpu.VMEM((BA * BB, LANES), F32),
            pltpu.VMEM((3, 2, 512, LANES), BF16),
            pltpu.VMEM((3, 1024, LANES), BF16),
            pltpu.VMEM((2, 512, LANES), BF16),
            pltpu.VMEM((2, 512, LANES), BF16),
            pltpu.VMEM((4, 2, ROWS // 2, LANES), BF16),
            pltpu.VMEM((4, 4, 2, 512, LANES), BF16),
            pltpu.VMEM((4, 2, 4, 1024, LANES), BF16),
            pltpu.VMEM((256, 1024), F32),
            pltpu.VMEM((8, 2, ROWS, LANES), BF16),
            pltpu.VMEM((4, 3, ROWS, LANES), BF16),
            pltpu.VMEM((NT * BA, LANES), F32),
            pltpu.VMEM((BA, BB, LANES), F32),
            pltpu.VMEM((2, BA, BA, LANES), BF16),
            pltpu.VMEM((2, 4, 3, 8, BA, LANES), BF16),
            pltpu.VMEM((2, BA, BA, LANES), BF16),
            pltpu.VMEM((2 * BA * BA, LANES), F32),
            dma((2, 4)), dma((2, 4)), dma((2, 2)), dma((2, 2)), dma((2, 2, 4)), dma((2, 2, 4)), dma((2, 2, 4)), dma((2, 2, 4)),
            dma((3, 4)), dma((3, 4)), dma((2, 4)), dma((2, 4)), dma((4, 6)), dma((4, 6)),
            dma((2, 4)), dma((2, 4, 3)), dma((2, 4, 3)), dma((2, 4)), dma((2, 4)), dma((6,)),
        ],
        compiler_params=pltpu.CompilerParams(collective_id=0, has_side_effects=True, vmem_limit_bytes=48 << 20),
        name="cycle",
    )(amplitudes, integrals)
    row_pos, col_pos = lax.axis_index("row"), lax.axis_index("col")
    vir_rows = lax.dynamic_slice_in_dim(vir_energy, row_pos * BA, BA).reshape(BA, 1, 1)
    vir_cols = lax.dynamic_slice_in_dim(vir_energy, col_pos * BB, BB).reshape(BB, 1)
    occ = (occ_energy[:, None] + occ_energy[None, :]).reshape(1, PAIRS)
    sel = jnp.asarray(spread_matrix(), BF16)
    return pl.pallas_call(
        update_kernel,
        grid=(BA // STEP,),
        out_shape=jax.ShapeDtypeStruct((BA, BB, PAIRS), F32),
        in_specs=[
            pl.BlockSpec((STEP, BB, PAIRS), lambda s: (s, 0, 0)),
            pl.BlockSpec((STEP, BB, LANES), lambda s: (s, 0, 0)),
            pl.BlockSpec((2 * LANES, PAIRS), lambda s: (0, 0)),
            pl.BlockSpec((1, PAIRS), lambda s: (0, 0)),
            pl.BlockSpec((STEP, 1, 1), lambda s: (s, 0, 0)),
            pl.BlockSpec((BB, 1), lambda s: (0, 0)),
        ],
        out_specs=pl.BlockSpec((STEP, BB, PAIRS), lambda s: (s, 0, 0)),
        compiler_params=pltpu.CompilerParams(vmem_limit_bytes=40 << 20),
        name="update",
    )(amplitudes, resid, sel, occ, vir_rows, vir_cols)


def solution(mesh):
    placed = (P("row", "col", None), P("row", "col", None), P(), P())
    return jax.shard_map(
        local, mesh=mesh, in_specs=placed, out_specs=P("row", "col", None), check_vma=False
    )
```

```python
import functools

import jax
import jax.numpy as jnp
import numpy as np
from jax import lax
from jax.experimental import pallas as pl
from jax.experimental.pallas import tpu as pltpu
from jax.sharding import PartitionSpec as P

OCC = 16
PAIRS = OCC * OCC
BA = 32
BB = 64
LANES = 128
F32, BF16 = jnp.float32, jnp.bfloat16
MESH = pl.DeviceIdType.MESH
VMEM = pl.BlockSpec(memory_space=pltpu.VMEM)
ANY = pl.BlockSpec(memory_space=pl.ANY)
TILES = [(i, jj) for i in range(OCC) for jj in range((i + 1) // 2, OCC // 2)]
NT = len(TILES)
STRAIGHT = {(0, 0), (0, 1), (0, 2), (0, 3), (1, 3)}
ROWS = NT * 8


def spread_matrix():
    sel = np.zeros((2, NT, OCC, OCC), np.float32)
    for t, (i, jj) in enumerate(TILES):
        for jp in range(2):
            j = 2 * jj + jp
            if j > i:
                sel[jp, t, i, j] = 1.0
                sel[jp, t, j, i] = -1.0
    sel = sel.reshape(2 * NT, PAIRS)
    return np.concatenate([sel, sel], 0)


def trade_chunks(blocks):
    lane = lax.broadcasted_iota(jnp.int32, blocks[0].shape, 1)
    blocks = list(blocks)
    for d in (4, 2, 1):
        upper = (lane & (16 * d)) != 0
        for c in range(8):
            if c & d:
                continue
            lo, hi = blocks[c], blocks[c + d]
            blocks[c] = jnp.where(upper, pltpu.roll(hi, 16 * d, 1), lo)
            blocks[c + d] = jnp.where(upper, hi, pltpu.roll(lo, LANES - 16 * d, 1))
    return blocks


def cycle_kernel(a_hbm, w_hbm, r_ref, av, wv, wide0, wide1, atb, wtb, ra, rw, rd, abuf, wbuf, cbuf, dsend, drecv, dsum, xf, xb, mid, ybuf, yf,
                 x_ss, x_rs, xf_ss, xf_rs, g_ss, g_rs, f_ss, f_rs, s_ss, s_rs, sf_ss, sf_rs, d_ss, d_rs, e_ss, e_rs, p_ss, m_ss, m_rs, l_sem):
    row, col = lax.axis_index("row"), lax.axis_index("col")
    z, xh, k = row // 4, lax.rem(row // 2, 2), lax.rem(row, 2)
    y, xl = col // 2, lax.rem(col, 2)
    x = xh * 2 + xl

    def at4(v, s):
        return lax.rem(v + (s + 4), 4)

    def dev(x, y, z, k):
        return (z * 4 + (x // 2) * 2 + k, y * 2 + lax.rem(x, 2))

    x_dev = [dev(at4(x, r), y, z, k) for r in range(4)]
    y_dev = [dev(x, at4(y, 1), z, k), dev(x, at4(y, -1), z, k)]
    z_dev = [dev(x, y, at4(z, 1), k), dev(x, y, at4(z, -1), k)]
    sib = dev(x, y, z, 1 - k)
    turned = xl * 2 + xh
    m_dev = [dev(turned, z, y, k), dev(turned, z, y, 1 - k)]
    diagonal = y == z
    own_turned = jnp.logical_and(diagonal, xh == xl)

    bar = pltpu.get_barrier_semaphore()

    def greet(d):
        pl.semaphore_signal(bar, inc=1, device_id=d, device_id_type=MESH)

    for d in x_dev[1:] + y_dev + z_dev + [sib]:
        greet(d)

    @pl.when(diagonal)
    def _():
        greet(m_dev[1])
        for j in range(1, 4):
            for d in (dev(turned, at4(y, j), z, k), dev(turned, y, at4(z, j), 1 - k),
                      dev(x, y, at4(z, j), k), dev(x, at4(y, j), z, k)):
                greet(d)

        @pl.when(jnp.logical_not(own_turned))
        def _():
            greet(m_dev[0])

    @pl.when(jnp.logical_not(diagonal))
    def _():
        for d in (dev(turned, z, z, k), dev(turned, y, y, 1 - k), dev(x, y, y, k), dev(x, z, z, k), m_dev[0], m_dev[1]):
            greet(d)

    load_a = pltpu.make_async_copy(a_hbm, av, l_sem.at[0])
    load_w = pltpu.make_async_copy(w_hbm, wv, l_sem.at[1])
    load_w.start()
    load_a.start()

    def remote(src, dst, ss, rs, to):
        return pltpu.make_async_remote_copy(
            src_ref=src, dst_ref=dst, send_sem=ss, recv_sem=rs, device_id=to, device_id_type=MESH)

    def arrived(ref, ss, rs):
        remote(ref, ref, ss, rs, sib).wait_recv()

    sends = []

    def go(*args):
        copy = remote(*args)
        copy.start()
        sends.append(copy)

    q = lax.broadcasted_iota(jnp.int32, (PAIRS, PAIRS), 0)
    r = lax.broadcasted_iota(jnp.int32, (PAIRS, PAIRS), 1)
    perm = jnp.where(((q >> 4) == (r & 15)) & ((q & 15) == (r >> 4)), 1.0, 0.0).astype(BF16)

    def arrange_w(share, out):
        wp = jnp.dot(wv[pl.ds(share * 8, 8)].reshape(8 * BB, PAIRS), perm, preferred_element_type=F32)
        for h in range(2):
            for s in range(2):
                blocks = [wp[c8 * BB + s * 32:c8 * BB + s * 32 + 32, h * LANES:(h + 1) * LANES] for c8 in range(8)]
                for j8, v in enumerate(trade_chunks(blocks)):
                    at = (h * 8 + j8) * BB + s * 32
                    out[at:at + 32, :] = v.astype(BF16)

    def arrange_a(share, out):
        for lo in range(2):
            for h, wide in enumerate((wide0, wide1)):
                blocks = [wide[pl.ds((share + 4 * lo) * 8 + c8, BA, stride=BB), :] for c8 in range(8)]
                for i8, v in enumerate(trade_chunks(blocks)):
                    at = (h * 8 + i8) * 16
                    v = v.astype(BF16)
                    out[lo, at:at + 16, :] = v[:16]
                    out[lo, 256 + at:256 + at + 16, :] = v[16:]

    load_w.wait()
    arrange_w(x, wbuf.at[z, k, x])

    @pl.when(jnp.logical_not(diagonal))
    def _():
        pl.semaphore_wait(bar, 14)

    @pl.when(own_turned)
    def _():
        pl.semaphore_wait(bar, 21)

    @pl.when(jnp.logical_and(diagonal, xh != xl))
    def _():
        pl.semaphore_wait(bar, 22)

    def ring_w(r):
        src = at4(x, -r)
        if r == 2:
            for d in range(2):
                half = wbuf.at[z, k, src, pl.ds(d * 512, 512)]
                arrived(half, xf_ss.at[1, d], xf_rs.at[1, d])
        elif r:
            arrived(wbuf.at[z, k, src], x_ss.at[1, r], x_rs.at[1, r])
        for d in range(2):
            go(wbuf.at[z, k, src], wbuf.at[z, k, src], g_ss.at[1, d, r], g_rs.at[1, d, r], z_dev[d])
        go(wbuf.at[z, k, src], wbuf.at[z, k, src], s_ss.at[0, r], s_rs.at[0, r], sib)

    def ring_a(r):
        src = at4(x, -r)
        if r == 2:
            for d in range(2):
                arrived(abuf.at[y, src, d], xf_ss.at[0, d], xf_rs.at[0, d])
        elif r:
            arrived(abuf.at[y, src], x_ss.at[0, r], x_rs.at[0, r])
        for d in range(2):
            go(abuf.at[y, src], abuf.at[y, src], g_ss.at[0, d, r], g_rs.at[0, d, r], y_dev[d])

    beside = [x_dev[1], x_dev[3]]

    def near_w(n, _):
        r = 2 * n - 1
        to = at4(x, r)
        arrange_w(to, wtb.at[n])
        remote(wtb.at[n], wbuf.at[z, k, x], x_ss.at[1, r], x_rs.at[1, r], dev(to, y, z, k)).start()
        return 0

    def near_a(n, _):
        r = 2 * n - 1
        to = at4(x, r)
        arrange_a(to, atb.at[n])
        remote(atb.at[n], abuf.at[y, x], x_ss.at[0, r], x_rs.at[0, r], dev(to, y, z, k)).start()
        return 0

    def stage_w():
        for d in range(2):
            go(wtb.at[0, pl.ds(d * 512, 512)], rw.at[d], x_ss.at[1, 2 * d], x_rs.at[1, 2 * d], beside[d])

    def stage_a():
        for d in range(2):
            go(atb.at[0, d], ra.at[d], x_ss.at[0, 2 * d], x_rs.at[0, 2 * d], beside[d])

    def relay_w():
        for d in range(2):
            arrived(rw.at[d], x_ss.at[1, 2 * d], x_rs.at[1, 2 * d])
            go(rw.at[d], wbuf.at[z, k, at4(x, 2 * d - 1), pl.ds(d * 512, 512)], xf_ss.at[1, d], xf_rs.at[1, d], beside[d])

    def relay_a():
        for d in range(2):
            arrived(ra.at[d], x_ss.at[0, 2 * d], x_rs.at[0, 2 * d])
            go(ra.at[d], abuf.at[y, at4(x, 2 * d - 1), d], xf_ss.at[0, d], xf_rs.at[0, d], beside[d])

    def forward_w(r):
        src = at4(x, -r)
        for d in range(2):
            zz = at4(z, 2 * d - 1)
            arrived(wbuf.at[zz, k, src], g_ss.at[1, d, r], g_rs.at[1, d, r])
            half = wbuf.at[zz, k, src, pl.ds(d * 512, 512)]
            go(half, half, f_ss.at[1, d, r], f_rs.at[1, d, r], z_dev[d])
            go(wbuf.at[zz, k, src], wbuf.at[zz, k, src], s_ss.at[1 + d, r], s_rs.at[1 + d, r], sib)

    def forward_a(r):
        src = at4(x, -r)
        for d in range(2):
            yy = at4(y, 2 * d - 1)
            arrived(abuf.at[yy, src], g_ss.at[0, d, r], g_rs.at[0, d, r])
            go(abuf.at[yy, src, d], abuf.at[yy, src, d], f_ss.at[0, d, r], f_rs.at[0, d, r], y_dev[d])

    def finish_w(r):
        for d in range(2):
            half = wbuf.at[at4(z, 2), k, at4(x, -r), pl.ds(d * 512, 512)]
            arrived(half, f_ss.at[1, d, r], f_rs.at[1, d, r])
            go(half, half, sf_ss.at[d, r], sf_rs.at[d, r], sib)

    def finish_a(r):
        for d in range(2):
            arrived(abuf.at[at4(y, 2), at4(x, -r), d], f_ss.at[0, d, r], f_rs.at[0, d, r])

    ring_w(0)
    lax.fori_loop(1, 3, near_w, 0)
    load_a.wait()
    for h, wide in enumerate((wide0, wide1)):
        wide[...] = av[:, :, h * LANES:(h + 1) * LANES].astype(F32).reshape(BA * BB, LANES)
    arrange_a(x, abuf.at[y, x])
    ring_a(0)
    lax.fori_loop(1, 3, near_a, 0)
    arrange_w(at4(x, 2), wtb.at[0])
    arrange_a(at4(x, 2), atb.at[0])
    forward_w(0)
    ring_w(1)
    ring_w(3)
    stage_w()
    forward_a(0)
    ring_a(1)
    ring_a(3)
    stage_a()
    forward_w(1)
    relay_w()
    forward_a(1)
    relay_a()
    ring_w(2)
    forward_w(3)
    ring_a(2)
    forward_a(3)
    finish_w(0)
    finish_w(1)
    forward_w(2)
    finish_w(3)
    forward_a(2)
    finish_w(2)
    for r in (0, 1, 3, 2):
        finish_a(r)
    for r in range(4):
        src = at4(x, -r)
        arrived(wbuf.at[z, 1 - k, src], s_ss.at[0, r], s_rs.at[0, r])
        for d in range(2):
            zz = at4(z, 2 * d - 1)
            arrived(wbuf.at[zz, 1 - k, src], s_ss.at[1 + d, r], s_rs.at[1 + d, r])
            arrived(wbuf.at[at4(z, 2), 1 - k, src, pl.ds(d * 512, 512)], sf_ss.at[d, r], sf_rs.at[d, r])

    left = lax.broadcasted_iota(jnp.int32, (16, LANES), 1) < BB

    def quadrant(n, _):
        h, s = n // 4, lax.rem(n, 4)
        to = lax.rem(x + 2 - s + 3 * (s // 2) + 2 * (s // 3), 4)
        th, tl = to // 2, lax.rem(to, 2)
        split = [(hi, mid, lo) for hi in range(4) for mid in range(2) for lo in range(2)]

        def columns(n, _):
            rows = pl.ds(pl.multiple_of(h * 256, 256), 256)
            lhs = jnp.concatenate([abuf[hi, 2 * th + mid, lo, rows] for hi, mid, lo in split], axis=1)
            rhs = jnp.concatenate([wbuf[hi, lo, 2 * mid + tl, pl.ds(n * 512, 512)] for hi, mid, lo in split], axis=1)
            cbuf[:, pl.ds(pl.multiple_of(n * 512, 512), 512)] = lax.dot_general(
                lhs, rhs, (((1,), (1,)), ((), ())), preferred_element_type=F32)
            return 0

        lax.fori_loop(0, 2, columns, 0)
        tiles = []
        for t, (i, jj) in enumerate(TILES):
            ii, ip = i // 2, i % 2
            here = cbuf[i * 16:(i + 1) * 16, jj * LANES:(jj + 1) * LANES]
            even = cbuf[2 * jj * 16:(2 * jj + 1) * 16, ii * LANES:(ii + 1) * LANES]
            odd = cbuf[(2 * jj + 1) * 16:(2 * jj + 2) * 16, ii * LANES:(ii + 1) * LANES]
            if ip == 0:
                other = jnp.where(left, even, pltpu.roll(odd, BB, 1))
            else:
                other = jnp.where(left, pltpu.roll(even, BB, 1), odd)
            tiles.append(here - other)
            if t % 2 == 0:
                continue
            for u in range(2):
                pair = jnp.concatenate([v[u * 8:u * 8 + 8] for v in tiles], axis=0)
                dsum[pl.ds((2 * h + u) * ROWS + (t - 1) * 8, 16), :] = pair
                dsend[n, u, (t - 1) * 8:(t + 1) * 8, :] = pair.astype(BF16)
            tiles = []

        @pl.when(s == 0)
        def _():
            stage_d(2 * h)

        @pl.when(lax.rem(s, 3) > 0)
        def _():
            near_d(2 * h, s)

        @pl.when(s == 3)
        def _():
            relay_d(2 * h)
            stage_d(2 * h + 1)
            near_d(2 * h + 1, 1)
            near_d(2 * h + 1, 2)

        @pl.when(n == 5)
        def _():
            relay_d(1)

        @pl.when(n == 6)
        def _():
            settle(0)
        return 0

    def term(c, s):
        return dsend.at[4 * (c // 2) + s, lax.rem(c, 2)]

    def d_copy(c, e, src, dst, to):
        return remote(src, dst, d_ss.at[c, e], d_rs.at[c, e], to)

    def stage_copy(c, d):
        return d_copy(c, d, term(c, 0).at[pl.ds(d * ROWS // 2, ROWS // 2)], rd.at[c, d], beside[d])

    def near_copy(c, s):
        return d_copy(c, s + 1, term(c, s), drecv.at[c, s], dev(at4(x, 3 - 2 * (2 - s)), y, z, k))

    def relay_copy(c, d):
        return d_copy(c, 4 + d, rd.at[c, d], drecv.at[c, 0, pl.ds(d * ROWS // 2, ROWS // 2)], beside[d])

    def stage_d(c):
        for d in range(2):
            stage_copy(c, d).start()

    def near_d(c, s):
        near_copy(c, s).start()

    def relay_d(c):
        for d in range(2):
            stage_copy(c, d).wait_recv()
            relay_copy(c, d).start()


    left2 = lax.broadcasted_iota(jnp.int32, (BB, LANES), 1) < BB

    def block(q, c):
        return xb.at[(k, 1 - k)[q], pl.ds(c * 8, 8)]

    def direct(q, c):
        return remote(block(q, c), ybuf.at[k, pl.ds(c * 8, 8)], m_ss.at[q, c], m_rs.at[q, c], m_dev[q])

    def same_chip(c):
        return pltpu.make_async_copy(block(0, c), ybuf.at[k, pl.ds(c * 8, 8)], l_sem.at[2 + c])

    def to_corner(q, c):
        if q == 0:
            corner, slot = dev(turned, z, z, k), lax.rem(y - z + 3, 4)
        else:
            corner, slot = dev(turned, y, y, 1 - k), lax.rem(z - y + 3, 4)
        return remote(block(q, c), mid.at[q, c, slot], e_ss.at[q, c], e_rs.at[q, c, slot], corner)

    def from_corner(q, c, j):
        there = dev(x, y, at4(z, 1 + j), k) if q == 0 else dev(x, at4(y, 1 + j), z, k)
        slot = k if q == 0 else 1 - k
        return remote(mid.at[q, c, j], ybuf.at[slot, pl.ds(c * 8, 8)], p_ss.at[q, c, j], m_rs.at[q, c], there)

    def pass_on(c):
        @pl.when(diagonal)
        def _():
            for q in range(2):
                if (q, c) in STRAIGHT:
                    continue

                def one(j, _):
                    arrived(mid.at[q, c, j], e_ss.at[q, c], e_rs.at[q, c, j])
                    from_corner(q, c, j).start()
                    return 0

                lax.fori_loop(0, 3, one, 0)

    def settle(c):
        for s in (1, 2):
            near_copy(c, s).wait_recv()
        for d in range(2):
            relay_copy(c, d).wait_recv()
        part = pl.ds(c * ROWS, ROWS)
        dsum[part, :] = dsum[part, :] + drecv[c, 0].astype(F32) + drecv[c, 1].astype(F32) + drecv[c, 2].astype(F32)

        def turn(p, _):
            rows = jnp.concatenate(
                [dsum[pl.ds(c * ROWS + 2 * p + q, NT, stride=8), :] for q in range(2)], axis=0)
            t = rows.T
            lo, hi = t[:BB], t[BB:]
            first = jnp.where(left2, lo, pltpu.roll(hi, BB, 1))
            second = jnp.where(left2, pltpu.roll(lo, BB, 1), hi)
            at = c * 8 + 2 * p
            xf[at] = first
            xf[at + 1] = second
            xb[0, at] = first[:BA].astype(BF16)
            xb[1, at] = first[BA:].astype(BF16)
            xb[0, at + 1] = second[:BA].astype(BF16)
            xb[1, at + 1] = second[BA:].astype(BF16)
            return 0

        lax.fori_loop(0, 4, turn, 0)

        @pl.when(jnp.logical_not(diagonal))
        def _():
            for q in range(2):
                (direct if (q, c) in STRAIGHT else to_corner)(q, c).start()

        @pl.when(diagonal)
        def _():
            direct(1, c).start()

            @pl.when(own_turned)
            def _():
                same_chip(c).start()

            @pl.when(jnp.logical_not(own_turned))
            def _():
                direct(0, c).start()


    lax.fori_loop(0, 8, quadrant, 0)
    relay_d(3)
    for c in range(1, 4):
        settle(c)
        pass_on(c - 1)
    pass_on(3)

    for c in range(4):
        @pl.when(own_turned)
        def _():
            same_chip(c).wait()

        @pl.when(jnp.logical_not(own_turned))
        def _():
            arrived(ybuf.at[k, pl.ds(c * 8, 8)], m_ss.at[0, c], m_rs.at[0, c])

        arrived(ybuf.at[1 - k, pl.ds(c * 8, 8)], m_ss.at[1, c], m_rs.at[1, c])
        for v in range(2):
            at = v * BA * BA + c * 8 * BA
            yf[at:at + 8 * BA, :] = ybuf[v, c * 8:c * 8 + 8].astype(F32).reshape(8 * BA, LANES)

    def mirror(a, _):
        r_ref[a] = xf[a] - yf[pl.ds(a, BB, stride=BA), :]
        return 0

    lax.fori_loop(0, BA, mirror, 0)
    for copy in sends:
        copy.wait_send()
    for n, r in ((1, 1), (2, 3)):
        remote(wtb.at[n], wbuf.at[z, k, x], x_ss.at[1, r], x_rs.at[1, r], sib).wait_send()
        remote(atb.at[n], abuf.at[y, x], x_ss.at[0, r], x_rs.at[0, r], sib).wait_send()
    for c in range(4):
        for s in (1, 2):
            near_copy(c, s).wait_send()
        for d in range(2):
            stage_copy(c, d).wait_send()
            relay_copy(c, d).wait_send()

        @pl.when(jnp.logical_not(diagonal))
        def _():
            for q in range(2):
                (direct if (q, c) in STRAIGHT else to_corner)(q, c).wait_send()

        @pl.when(diagonal)
        def _():
            direct(1, c).wait_send()
            for q in range(2):
                if (q, c) not in STRAIGHT:
                    for j in range(3):
                        from_corner(q, c, j).wait_send()

            @pl.when(jnp.logical_not(own_turned))
            def _():
                direct(0, c).wait_send()


STEP = 8


def update_kernel(a_ref, r_ref, sel_ref, occ_ref, vrow_ref, vcol_ref, o_ref):
    r = r_ref[...].reshape(STEP * BB, LANES)
    hi = r.astype(BF16)
    lo = (r - hi.astype(F32)).astype(BF16)
    full = jnp.dot(jnp.concatenate([hi, lo], axis=1), sel_ref[...], preferred_element_type=F32)
    lane = lax.broadcasted_iota(jnp.int32, (1, PAIRS), 1)
    occ_i, occ_j = jnp.zeros((1, PAIRS), F32), jnp.zeros((1, PAIRS), F32)
    for n in range(OCC):
        occ_i = jnp.where((lane >> 4) == n, occ_ref[n], occ_i)
        occ_j = jnp.where((lane & 15) == n, occ_ref[n], occ_j)
    den = ((occ_i + occ_j)[None] - vrow_ref[...]) - vcol_ref[...][None]
    o_ref[...] = a_ref[...].astype(F32) + full.reshape(STEP, BB, PAIRS) / den


def local(amplitudes, integrals, occ_energy, vir_energy):
    dma = pltpu.SemaphoreType.DMA
    resid = pl.pallas_call(
        cycle_kernel,
        out_shape=jax.ShapeDtypeStruct((BA, BB, LANES), F32),
        in_specs=[ANY, ANY],
        out_specs=VMEM,
        scratch_shapes=[
            pltpu.VMEM((BA, BB, PAIRS), BF16),
            pltpu.VMEM((BA, BB, PAIRS), BF16),
            pltpu.VMEM((BA * BB, LANES), F32),
            pltpu.VMEM((BA * BB, LANES), F32),
            pltpu.VMEM((3, 2, 512, LANES), BF16),
            pltpu.VMEM((3, 1024, LANES), BF16),
            pltpu.VMEM((2, 512, LANES), BF16),
            pltpu.VMEM((2, 512, LANES), BF16),
            pltpu.VMEM((4, 2, ROWS // 2, LANES), BF16),
            pltpu.VMEM((4, 4, 2, 512, LANES), BF16),
            pltpu.VMEM((4, 2, 4, 1024, LANES), BF16),
            pltpu.VMEM((256, 1024), F32),
            pltpu.VMEM((8, 2, ROWS, LANES), BF16),
            pltpu.VMEM((4, 3, ROWS, LANES), BF16),
            pltpu.VMEM((NT * BA, LANES), F32),
            pltpu.VMEM((BA, BB, LANES), F32),
            pltpu.VMEM((2, BA, BA, LANES), BF16),
            pltpu.VMEM((2, 4, 3, 8, BA, LANES), BF16),
            pltpu.VMEM((2, BA, BA, LANES), BF16),
            pltpu.VMEM((2 * BA * BA, LANES), F32),
            dma((2, 4)), dma((2, 4)), dma((2, 2)), dma((2, 2)), dma((2, 2, 4)), dma((2, 2, 4)), dma((2, 2, 4)), dma((2, 2, 4)),
            dma((3, 4)), dma((3, 4)), dma((2, 4)), dma((2, 4)), dma((4, 6)), dma((4, 6)),
            dma((2, 4)), dma((2, 4, 3)), dma((2, 4, 3)), dma((2, 4)), dma((2, 4)), dma((6,)),
        ],
        compiler_params=pltpu.CompilerParams(collective_id=0, has_side_effects=True, vmem_limit_bytes=48 << 20),
        name="cycle",
    )(amplitudes, integrals)
    row_pos, col_pos = lax.axis_index("row"), lax.axis_index("col")
    vir_rows = lax.dynamic_slice_in_dim(vir_energy, row_pos * BA, BA).reshape(BA, 1, 1)
    vir_cols = lax.dynamic_slice_in_dim(vir_energy, col_pos * BB, BB).reshape(BB, 1)
    sel = jnp.asarray(spread_matrix(), BF16)
    return pl.pallas_call(
        update_kernel,
        grid=(BA // STEP,),
        out_shape=jax.ShapeDtypeStruct((BA, BB, PAIRS), F32),
        in_specs=[
            pl.BlockSpec((STEP, BB, PAIRS), lambda s: (s, 0, 0)),
            pl.BlockSpec((STEP, BB, LANES), lambda s: (s, 0, 0)),
            pl.BlockSpec((2 * LANES, PAIRS), lambda s: (0, 0)),
            pl.BlockSpec(memory_space=pltpu.SMEM),
            pl.BlockSpec((STEP, 1, 1), lambda s: (s, 0, 0)),
            pl.BlockSpec((BB, 1), lambda s: (0, 0)),
        ],
        out_specs=pl.BlockSpec((STEP, BB, PAIRS), lambda s: (s, 0, 0)),
        compiler_params=pltpu.CompilerParams(vmem_limit_bytes=40 << 20),
        name="update",
    )(amplitudes, resid, sel, occ_energy, vir_rows, vir_cols)


def solution(mesh):
    placed = (P("row", "col", None), P("row", "col", None), P(), P())
    return jax.shard_map(
        local, mesh=mesh, in_specs=placed, out_specs=P("row", "col", None), check_vma=False
    )
```

```python
import functools

import jax
import jax.numpy as jnp
import numpy as np
from jax import lax
from jax.experimental import pallas as pl
from jax.experimental.pallas import tpu as pltpu
from jax.sharding import PartitionSpec as P

OCC = 16
PAIRS = OCC * OCC
BA = 32
BB = 64
LANES = 128
F32, BF16 = jnp.float32, jnp.bfloat16
MESH = pl.DeviceIdType.MESH
VMEM = pl.BlockSpec(memory_space=pltpu.VMEM)
ANY = pl.BlockSpec(memory_space=pl.ANY)
TILES = [(i, jj) for i in range(OCC) for jj in range((i + 1) // 2, OCC // 2)]
NT = len(TILES)
STRAIGHT = {(0, 0), (0, 1), (0, 2), (0, 3), (1, 3)}
ROWS = NT * 8


def spread_matrix():
    sel = np.zeros((2, NT, OCC, OCC), np.float32)
    for t, (i, jj) in enumerate(TILES):
        for jp in range(2):
            j = 2 * jj + jp
            if j > i:
                sel[jp, t, i, j] = 1.0
                sel[jp, t, j, i] = -1.0
    sel = sel.reshape(2 * NT, PAIRS)
    return np.concatenate([sel, sel], 0)


def trade_chunks(blocks):
    lane = lax.broadcasted_iota(jnp.int32, blocks[0].shape, 1)
    blocks = list(blocks)
    for d in (4, 2, 1):
        upper = (lane & (16 * d)) != 0
        for c in range(8):
            if c & d:
                continue
            lo, hi = blocks[c], blocks[c + d]
            blocks[c] = jnp.where(upper, pltpu.roll(hi, 16 * d, 1), lo)
            blocks[c + d] = jnp.where(upper, hi, pltpu.roll(lo, LANES - 16 * d, 1))
    return blocks


def cycle_kernel(a_hbm, w_hbm, r_ref, av, wv, wide0, wide1, atb, wtb, ra, rw, rd, abuf, wbuf, cbuf, dsend, drecv, dsum, xf, xb, mid, ybuf, yf,
                 x_ss, x_rs, xf_ss, xf_rs, g_ss, g_rs, f_ss, f_rs, s_ss, s_rs, sf_ss, sf_rs, d_ss, d_rs, e_ss, e_rs, p_ss, m_ss, m_rs, l_sem):
    row, col = lax.axis_index("row"), lax.axis_index("col")
    z, xh, k = row // 4, lax.rem(row // 2, 2), lax.rem(row, 2)
    y, xl = col // 2, lax.rem(col, 2)
    x = xh * 2 + xl

    def at4(v, s):
        return lax.rem(v + (s + 4), 4)

    def dev(x, y, z, k):
        return (z * 4 + (x // 2) * 2 + k, y * 2 + lax.rem(x, 2))

    x_dev = [dev(at4(x, r), y, z, k) for r in range(4)]
    y_dev = [dev(x, at4(y, 1), z, k), dev(x, at4(y, -1), z, k)]
    z_dev = [dev(x, y, at4(z, 1), k), dev(x, y, at4(z, -1), k)]
    sib = dev(x, y, z, 1 - k)
    turned = xl * 2 + xh
    m_dev = [dev(turned, z, y, k), dev(turned, z, y, 1 - k)]
    diagonal = y == z
    own_turned = jnp.logical_and(diagonal, xh == xl)

    bar = pltpu.get_barrier_semaphore()

    def greet(d):
        pl.semaphore_signal(bar, inc=1, device_id=d, device_id_type=MESH)

    for d in x_dev[1:] + y_dev + z_dev + [sib]:
        greet(d)

    @pl.when(diagonal)
    def _():
        greet(m_dev[1])
        for j in range(1, 4):
            for d in (dev(turned, at4(y, j), z, k), dev(turned, y, at4(z, j), 1 - k),
                      dev(x, y, at4(z, j), k), dev(x, at4(y, j), z, k)):
                greet(d)

        @pl.when(jnp.logical_not(own_turned))
        def _():
            greet(m_dev[0])

    @pl.when(jnp.logical_not(diagonal))
    def _():
        for d in (dev(turned, z, z, k), dev(turned, y, y, 1 - k), dev(x, y, y, k), dev(x, z, z, k), m_dev[0], m_dev[1]):
            greet(d)

    load_a = pltpu.make_async_copy(a_hbm, av, l_sem.at[0])
    load_w = pltpu.make_async_copy(w_hbm, wv, l_sem.at[1])
    load_w.start()
    load_a.start()

    def remote(src, dst, ss, rs, to):
        return pltpu.make_async_remote_copy(
            src_ref=src, dst_ref=dst, send_sem=ss, recv_sem=rs, device_id=to, device_id_type=MESH)

    def arrived(ref, ss, rs):
        remote(ref, ref, ss, rs, sib).wait_recv()

    sends = []

    def go(*args):
        copy = remote(*args)
        copy.start()
        sends.append(copy)

    q = lax.broadcasted_iota(jnp.int32, (PAIRS, PAIRS), 0)
    r = lax.broadcasted_iota(jnp.int32, (PAIRS, PAIRS), 1)
    perm = jnp.where(((q >> 4) == (r & 15)) & ((q & 15) == (r >> 4)), 1.0, 0.0).astype(BF16)

    def arrange_w(share, out):
        wp = jnp.dot(wv[pl.ds(share * 8, 8)].reshape(8 * BB, PAIRS), perm, preferred_element_type=F32)
        for h in range(2):
            for s in range(2):
                blocks = [wp[c8 * BB + s * 32:c8 * BB + s * 32 + 32, h * LANES:(h + 1) * LANES] for c8 in range(8)]
                for j8, v in enumerate(trade_chunks(blocks)):
                    at = (h * 8 + j8) * BB + s * 32
                    out[at:at + 32, :] = v.astype(BF16)

    def arrange_a(share, out):
        for lo in range(2):
            for h, wide in enumerate((wide0, wide1)):
                blocks = [wide[pl.ds((share + 4 * lo) * 8 + c8, BA, stride=BB), :] for c8 in range(8)]
                for i8, v in enumerate(trade_chunks(blocks)):
                    at = (h * 8 + i8) * 16
                    v = v.astype(BF16)
                    out[lo, at:at + 16, :] = v[:16]
                    out[lo, 256 + at:256 + at + 16, :] = v[16:]

    load_w.wait()
    arrange_w(x, wbuf.at[z, k, x])

    @pl.when(jnp.logical_not(diagonal))
    def _():
        pl.semaphore_wait(bar, 14)

    @pl.when(own_turned)
    def _():
        pl.semaphore_wait(bar, 21)

    @pl.when(jnp.logical_and(diagonal, xh != xl))
    def _():
        pl.semaphore_wait(bar, 22)

    def ring_w(r):
        src = at4(x, -r)
        if r == 2:
            for d in range(2):
                half = wbuf.at[z, k, src, pl.ds(d * 512, 512)]
                arrived(half, xf_ss.at[1, d], xf_rs.at[1, d])
        elif r:
            arrived(wbuf.at[z, k, src], x_ss.at[1, r], x_rs.at[1, r])
        for d in range(2):
            go(wbuf.at[z, k, src], wbuf.at[z, k, src], g_ss.at[1, d, r], g_rs.at[1, d, r], z_dev[d])
        go(wbuf.at[z, k, src], wbuf.at[z, k, src], s_ss.at[0, r], s_rs.at[0, r], sib)

    def ring_a(r):
        src = at4(x, -r)
        if r == 2:
            for d in range(2):
                arrived(abuf.at[y, src, d], xf_ss.at[0, d], xf_rs.at[0, d])
        elif r:
            arrived(abuf.at[y, src], x_ss.at[0, r], x_rs.at[0, r])
        for d in range(2):
            go(abuf.at[y, src], abuf.at[y, src], g_ss.at[0, d, r], g_rs.at[0, d, r], y_dev[d])

    beside = [x_dev[1], x_dev[3]]

    def near_w(n, _):
        r = 2 * n - 1
        to = at4(x, r)
        arrange_w(to, wtb.at[n])
        remote(wtb.at[n], wbuf.at[z, k, x], x_ss.at[1, r], x_rs.at[1, r], dev(to, y, z, k)).start()
        return 0

    def near_a(n, _):
        r = 2 * n - 1
        to = at4(x, r)
        arrange_a(to, atb.at[n])
        remote(atb.at[n], abuf.at[y, x], x_ss.at[0, r], x_rs.at[0, r], dev(to, y, z, k)).start()
        return 0

    def stage_w():
        for d in range(2):
            go(wtb.at[0, pl.ds(d * 512, 512)], rw.at[d], x_ss.at[1, 2 * d], x_rs.at[1, 2 * d], beside[d])

    def stage_a():
        for d in range(2):
            go(atb.at[0, d], ra.at[d], x_ss.at[0, 2 * d], x_rs.at[0, 2 * d], beside[d])

    def relay_w():
        for d in range(2):
            arrived(rw.at[d], x_ss.at[1, 2 * d], x_rs.at[1, 2 * d])
            go(rw.at[d], wbuf.at[z, k, at4(x, 2 * d - 1), pl.ds(d * 512, 512)], xf_ss.at[1, d], xf_rs.at[1, d], beside[d])

    def relay_a():
        for d in range(2):
            arrived(ra.at[d], x_ss.at[0, 2 * d], x_rs.at[0, 2 * d])
            go(ra.at[d], abuf.at[y, at4(x, 2 * d - 1), d], xf_ss.at[0, d], xf_rs.at[0, d], beside[d])

    def forward_w(r):
        src = at4(x, -r)
        for d in range(2):
            zz = at4(z, 2 * d - 1)
            arrived(wbuf.at[zz, k, src], g_ss.at[1, d, r], g_rs.at[1, d, r])
            half = wbuf.at[zz, k, src, pl.ds(d * 512, 512)]
            go(half, half, f_ss.at[1, d, r], f_rs.at[1, d, r], z_dev[d])
            go(wbuf.at[zz, k, src], wbuf.at[zz, k, src], s_ss.at[1 + d, r], s_rs.at[1 + d, r], sib)

    def forward_a(r):
        src = at4(x, -r)
        for d in range(2):
            yy = at4(y, 2 * d - 1)
            arrived(abuf.at[yy, src], g_ss.at[0, d, r], g_rs.at[0, d, r])
            go(abuf.at[yy, src, d], abuf.at[yy, src, d], f_ss.at[0, d, r], f_rs.at[0, d, r], y_dev[d])

    def finish_w(r):
        for d in range(2):
            half = wbuf.at[at4(z, 2), k, at4(x, -r), pl.ds(d * 512, 512)]
            arrived(half, f_ss.at[1, d, r], f_rs.at[1, d, r])
            go(half, half, sf_ss.at[d, r], sf_rs.at[d, r], sib)

    def finish_a(r):
        for d in range(2):
            arrived(abuf.at[at4(y, 2), at4(x, -r), d], f_ss.at[0, d, r], f_rs.at[0, d, r])

    ring_w(0)
    lax.fori_loop(1, 3, near_w, 0)
    load_a.wait()
    for h, wide in enumerate((wide0, wide1)):
        wide[...] = av[:, :, h * LANES:(h + 1) * LANES].astype(F32).reshape(BA * BB, LANES)
    arrange_a(x, abuf.at[y, x])
    ring_a(0)
    lax.fori_loop(1, 3, near_a, 0)
    arrange_w(at4(x, 2), wtb.at[0])
    arrange_a(at4(x, 2), atb.at[0])
    forward_w(0)
    ring_w(1)
    ring_w(3)
    stage_w()
    forward_a(0)
    ring_a(1)
    ring_a(3)
    stage_a()
    forward_w(1)
    relay_w()
    forward_a(1)
    relay_a()
    ring_w(2)
    forward_w(3)
    ring_a(2)
    forward_a(3)
    finish_w(0)
    finish_w(1)
    forward_w(2)
    finish_w(3)
    forward_a(2)
    finish_w(2)
    for r in (0, 1, 3, 2):
        finish_a(r)
    for r in range(4):
        src = at4(x, -r)
        arrived(wbuf.at[z, 1 - k, src], s_ss.at[0, r], s_rs.at[0, r])
        for d in range(2):
            zz = at4(z, 2 * d - 1)
            arrived(wbuf.at[zz, 1 - k, src], s_ss.at[1 + d, r], s_rs.at[1 + d, r])
            arrived(wbuf.at[at4(z, 2), 1 - k, src, pl.ds(d * 512, 512)], sf_ss.at[d, r], sf_rs.at[d, r])

    left = lax.broadcasted_iota(jnp.int32, (16, LANES), 1) < BB

    def quadrant(n, _):
        h, s = n // 4, lax.rem(n, 4)
        to = lax.rem(x + 2 - s + 3 * (s // 2) + 2 * (s // 3), 4)
        th, tl = to // 2, lax.rem(to, 2)
        split = [(hi, mid, lo) for hi in range(4) for mid in range(2) for lo in range(2)]

        def columns(n, _):
            rows = pl.ds(pl.multiple_of(h * 256, 256), 256)
            lhs = jnp.concatenate([abuf[hi, 2 * th + mid, lo, rows] for hi, mid, lo in split], axis=1)
            rhs = jnp.concatenate([wbuf[hi, lo, 2 * mid + tl, pl.ds(n, 1024)] for hi, mid, lo in split], axis=1)
            cbuf[...] = lax.dot_general(
                lhs, rhs, (((1,), (1,)), ((), ())), preferred_element_type=F32)
            return 0

        columns(0, 0)
        tiles = []
        for t, (i, jj) in enumerate(TILES):
            ii, ip = i // 2, i % 2
            here = cbuf[i * 16:(i + 1) * 16, jj * LANES:(jj + 1) * LANES]
            even = cbuf[2 * jj * 16:(2 * jj + 1) * 16, ii * LANES:(ii + 1) * LANES]
            odd = cbuf[(2 * jj + 1) * 16:(2 * jj + 2) * 16, ii * LANES:(ii + 1) * LANES]
            if ip == 0:
                other = jnp.where(left, even, pltpu.roll(odd, BB, 1))
            else:
                other = jnp.where(left, pltpu.roll(even, BB, 1), odd)
            tiles.append(here - other)
            if t % 2 == 0:
                continue
            for u in range(2):
                pair = jnp.concatenate([v[u * 8:u * 8 + 8] for v in tiles], axis=0)
                dsum[pl.ds((2 * h + u) * ROWS + (t - 1) * 8, 16), :] = pair
                dsend[n, u, (t - 1) * 8:(t + 1) * 8, :] = pair.astype(BF16)
            tiles = []

        @pl.when(s == 0)
        def _():
            stage_d(2 * h)

        @pl.when(lax.rem(s, 3) > 0)
        def _():
            near_d(2 * h, s)

        @pl.when(s == 3)
        def _():
            relay_d(2 * h)
            stage_d(2 * h + 1)
            near_d(2 * h + 1, 1)
            near_d(2 * h + 1, 2)

        @pl.when(n == 5)
        def _():
            relay_d(1)

        @pl.when(n == 6)
        def _():
            settle(0)
        return 0

    def term(c, s):
        return dsend.at[4 * (c // 2) + s, lax.rem(c, 2)]

    def d_copy(c, e, src, dst, to):
        return remote(src, dst, d_ss.at[c, e], d_rs.at[c, e], to)

    def stage_copy(c, d):
        return d_copy(c, d, term(c, 0).at[pl.ds(d * ROWS // 2, ROWS // 2)], rd.at[c, d], beside[d])

    def near_copy(c, s):
        return d_copy(c, s + 1, term(c, s), drecv.at[c, s], dev(at4(x, 3 - 2 * (2 - s)), y, z, k))

    def relay_copy(c, d):
        return d_copy(c, 4 + d, rd.at[c, d], drecv.at[c, 0, pl.ds(d * ROWS // 2, ROWS // 2)], beside[d])

    def stage_d(c):
        for d in range(2):
            stage_copy(c, d).start()

    def near_d(c, s):
        near_copy(c, s).start()

    def relay_d(c):
        for d in range(2):
            stage_copy(c, d).wait_recv()
            relay_copy(c, d).start()


    left2 = lax.broadcasted_iota(jnp.int32, (BB, LANES), 1) < BB

    def block(q, c):
        return xb.at[(k, 1 - k)[q], pl.ds(c * 8, 8)]

    def direct(q, c):
        return remote(block(q, c), ybuf.at[k, pl.ds(c * 8, 8)], m_ss.at[q, c], m_rs.at[q, c], m_dev[q])

    def same_chip(c):
        return pltpu.make_async_copy(block(0, c), ybuf.at[k, pl.ds(c * 8, 8)], l_sem.at[2 + c])

    def to_corner(q, c):
        if q == 0:
            corner, slot = dev(turned, z, z, k), lax.rem(y - z + 3, 4)
        else:
            corner, slot = dev(turned, y, y, 1 - k), lax.rem(z - y + 3, 4)
        return remote(block(q, c), mid.at[q, c, slot], e_ss.at[q, c], e_rs.at[q, c, slot], corner)

    def from_corner(q, c, j):
        there = dev(x, y, at4(z, 1 + j), k) if q == 0 else dev(x, at4(y, 1 + j), z, k)
        slot = k if q == 0 else 1 - k
        return remote(mid.at[q, c, j], ybuf.at[slot, pl.ds(c * 8, 8)], p_ss.at[q, c, j], m_rs.at[q, c], there)

    def pass_on(c):
        @pl.when(diagonal)
        def _():
            for q in range(2):
                if (q, c) in STRAIGHT:
                    continue

                def one(j, _):
                    arrived(mid.at[q, c, j], e_ss.at[q, c], e_rs.at[q, c, j])
                    from_corner(q, c, j).start()
                    return 0

                lax.fori_loop(0, 3, one, 0)

    def settle(c):
        for s in (1, 2):
            near_copy(c, s).wait_recv()
        for d in range(2):
            relay_copy(c, d).wait_recv()
        part = pl.ds(c * ROWS, ROWS)
        dsum[part, :] = dsum[part, :] + drecv[c, 0].astype(F32) + drecv[c, 1].astype(F32) + drecv[c, 2].astype(F32)

        def turn(p, _):
            rows = jnp.concatenate(
                [dsum[pl.ds(c * ROWS + 2 * p + q, NT, stride=8), :] for q in range(2)], axis=0)
            t = rows.T
            lo, hi = t[:BB], t[BB:]
            first = jnp.where(left2, lo, pltpu.roll(hi, BB, 1))
            second = jnp.where(left2, pltpu.roll(lo, BB, 1), hi)
            at = c * 8 + 2 * p
            xf[at] = first
            xf[at + 1] = second
            xb[0, at] = first[:BA].astype(BF16)
            xb[1, at] = first[BA:].astype(BF16)
            xb[0, at + 1] = second[:BA].astype(BF16)
            xb[1, at + 1] = second[BA:].astype(BF16)
            return 0

        lax.fori_loop(0, 4, turn, 0)

        @pl.when(jnp.logical_not(diagonal))
        def _():
            for q in range(2):
                (direct if (q, c) in STRAIGHT else to_corner)(q, c).start()

        @pl.when(diagonal)
        def _():
            direct(1, c).start()

            @pl.when(own_turned)
            def _():
                same_chip(c).start()

            @pl.when(jnp.logical_not(own_turned))
            def _():
                direct(0, c).start()


    lax.fori_loop(0, 8, quadrant, 0)
    relay_d(3)
    for c in range(1, 4):
        settle(c)
        pass_on(c - 1)
    pass_on(3)

    for c in range(4):
        @pl.when(own_turned)
        def _():
            same_chip(c).wait()

        @pl.when(jnp.logical_not(own_turned))
        def _():
            arrived(ybuf.at[k, pl.ds(c * 8, 8)], m_ss.at[0, c], m_rs.at[0, c])

        arrived(ybuf.at[1 - k, pl.ds(c * 8, 8)], m_ss.at[1, c], m_rs.at[1, c])
        for v in range(2):
            at = v * BA * BA + c * 8 * BA
            yf[at:at + 8 * BA, :] = ybuf[v, c * 8:c * 8 + 8].astype(F32).reshape(8 * BA, LANES)

    def mirror(a, _):
        r_ref[a] = xf[a] - yf[pl.ds(a, BB, stride=BA), :]
        return 0

    lax.fori_loop(0, BA, mirror, 0)
    for copy in sends:
        copy.wait_send()
    for n, r in ((1, 1), (2, 3)):
        remote(wtb.at[n], wbuf.at[z, k, x], x_ss.at[1, r], x_rs.at[1, r], sib).wait_send()
        remote(atb.at[n], abuf.at[y, x], x_ss.at[0, r], x_rs.at[0, r], sib).wait_send()
    for c in range(4):
        for s in (1, 2):
            near_copy(c, s).wait_send()
        for d in range(2):
            stage_copy(c, d).wait_send()
            relay_copy(c, d).wait_send()

        @pl.when(jnp.logical_not(diagonal))
        def _():
            for q in range(2):
                (direct if (q, c) in STRAIGHT else to_corner)(q, c).wait_send()

        @pl.when(diagonal)
        def _():
            direct(1, c).wait_send()
            for q in range(2):
                if (q, c) not in STRAIGHT:
                    for j in range(3):
                        from_corner(q, c, j).wait_send()

            @pl.when(jnp.logical_not(own_turned))
            def _():
                direct(0, c).wait_send()


STEP = 8


def update_kernel(a_ref, r_ref, sel_ref, occ_ref, vrow_ref, vcol_ref, o_ref):
    r = r_ref[...].reshape(STEP * BB, LANES)
    hi = r.astype(BF16)
    lo = (r - hi.astype(F32)).astype(BF16)
    full = jnp.dot(jnp.concatenate([hi, lo], axis=1), sel_ref[...], preferred_element_type=F32)
    lane = lax.broadcasted_iota(jnp.int32, (1, PAIRS), 1)
    occ_i, occ_j = jnp.zeros((1, PAIRS), F32), jnp.zeros((1, PAIRS), F32)
    for n in range(OCC):
        occ_i = jnp.where((lane >> 4) == n, occ_ref[n], occ_i)
        occ_j = jnp.where((lane & 15) == n, occ_ref[n], occ_j)
    den = ((occ_i + occ_j)[None] - vrow_ref[...]) - vcol_ref[...][None]
    o_ref[...] = a_ref[...].astype(F32) + full.reshape(STEP, BB, PAIRS) / den


def local(amplitudes, integrals, occ_energy, vir_energy):
    dma = pltpu.SemaphoreType.DMA
    resid = pl.pallas_call(
        cycle_kernel,
        out_shape=jax.ShapeDtypeStruct((BA, BB, LANES), F32),
        in_specs=[ANY, ANY],
        out_specs=VMEM,
        scratch_shapes=[
            pltpu.VMEM((BA, BB, PAIRS), BF16),
            pltpu.VMEM((BA, BB, PAIRS), BF16),
            pltpu.VMEM((BA * BB, LANES), F32),
            pltpu.VMEM((BA * BB, LANES), F32),
            pltpu.VMEM((3, 2, 512, LANES), BF16),
            pltpu.VMEM((3, 1024, LANES), BF16),
            pltpu.VMEM((2, 512, LANES), BF16),
            pltpu.VMEM((2, 512, LANES), BF16),
            pltpu.VMEM((4, 2, ROWS // 2, LANES), BF16),
            pltpu.VMEM((4, 4, 2, 512, LANES), BF16),
            pltpu.VMEM((4, 2, 4, 1024, LANES), BF16),
            pltpu.VMEM((256, 1024), F32),
            pltpu.VMEM((8, 2, ROWS, LANES), BF16),
            pltpu.VMEM((4, 3, ROWS, LANES), BF16),
            pltpu.VMEM((NT * BA, LANES), F32),
            pltpu.VMEM((BA, BB, LANES), F32),
            pltpu.VMEM((2, BA, BA, LANES), BF16),
            pltpu.VMEM((2, 4, 3, 8, BA, LANES), BF16),
            pltpu.VMEM((2, BA, BA, LANES), BF16),
            pltpu.VMEM((2 * BA * BA, LANES), F32),
            dma((2, 4)), dma((2, 4)), dma((2, 2)), dma((2, 2)), dma((2, 2, 4)), dma((2, 2, 4)), dma((2, 2, 4)), dma((2, 2, 4)),
            dma((3, 4)), dma((3, 4)), dma((2, 4)), dma((2, 4)), dma((4, 6)), dma((4, 6)),
            dma((2, 4)), dma((2, 4, 3)), dma((2, 4, 3)), dma((2, 4)), dma((2, 4)), dma((6,)),
        ],
        compiler_params=pltpu.CompilerParams(collective_id=0, has_side_effects=True, vmem_limit_bytes=48 << 20),
        name="cycle",
    )(amplitudes, integrals)
    row_pos, col_pos = lax.axis_index("row"), lax.axis_index("col")
    vir_rows = lax.dynamic_slice_in_dim(vir_energy, row_pos * BA, BA).reshape(BA, 1, 1)
    vir_cols = lax.dynamic_slice_in_dim(vir_energy, col_pos * BB, BB).reshape(BB, 1)
    sel = jnp.asarray(spread_matrix(), BF16)
    return pl.pallas_call(
        update_kernel,
        grid=(BA // STEP,),
        out_shape=jax.ShapeDtypeStruct((BA, BB, PAIRS), F32),
        in_specs=[
            pl.BlockSpec((STEP, BB, PAIRS), lambda s: (s, 0, 0)),
            pl.BlockSpec((STEP, BB, LANES), lambda s: (s, 0, 0)),
            pl.BlockSpec((2 * LANES, PAIRS), lambda s: (0, 0)),
            pl.BlockSpec(memory_space=pltpu.SMEM),
            pl.BlockSpec((STEP, 1, 1), lambda s: (s, 0, 0)),
            pl.BlockSpec((BB, 1), lambda s: (0, 0)),
        ],
        out_specs=pl.BlockSpec((STEP, BB, PAIRS), lambda s: (s, 0, 0)),
        compiler_params=pltpu.CompilerParams(vmem_limit_bytes=40 << 20),
        name="update",
    )(amplitudes, resid, sel, occ_energy, vir_rows, vir_cols)


def solution(mesh):
    placed = (P("row", "col", None), P("row", "col", None), P(), P())
    return jax.shard_map(
        local, mesh=mesh, in_specs=placed, out_specs=P("row", "col", None), check_vma=False
    )
```

```python
import functools

import jax
import jax.numpy as jnp
import numpy as np
from jax import lax
from jax.experimental import pallas as pl
from jax.experimental.pallas import tpu as pltpu
from jax.sharding import PartitionSpec as P

OCC = 16
PAIRS = OCC * OCC
BA = 32
BB = 64
LANES = 128
F32, BF16 = jnp.float32, jnp.bfloat16
MESH = pl.DeviceIdType.MESH
VMEM = pl.BlockSpec(memory_space=pltpu.VMEM)
ANY = pl.BlockSpec(memory_space=pl.ANY)
TILES = [(i, jj) for i in range(OCC) for jj in range((i + 1) // 2, OCC // 2)]
NT = len(TILES)
STRAIGHT = {(0, 0), (0, 1), (0, 2), (0, 3), (1, 3)}
ROWS = NT * 8


def spread_matrix():
    sel = np.zeros((2, NT, OCC, OCC), np.float32)
    for t, (i, jj) in enumerate(TILES):
        for jp in range(2):
            j = 2 * jj + jp
            if j > i:
                sel[jp, t, i, j] = 1.0
                sel[jp, t, j, i] = -1.0
    sel = sel.reshape(2 * NT, PAIRS)
    return np.concatenate([sel, sel], 0)


def trade_chunks(blocks):
    lane = lax.broadcasted_iota(jnp.int32, blocks[0].shape, 1)
    blocks = list(blocks)
    for d in (4, 2, 1):
        upper = (lane & (16 * d)) != 0
        for c in range(8):
            if c & d:
                continue
            lo, hi = blocks[c], blocks[c + d]
            blocks[c] = jnp.where(upper, pltpu.roll(hi, 16 * d, 1), lo)
            blocks[c + d] = jnp.where(upper, hi, pltpu.roll(lo, LANES - 16 * d, 1))
    return blocks


def cycle_kernel(a_hbm, w_hbm, r_ref, av, wv, wide0, wide1, atb, wtb, ra, rw, rd, abuf, wbuf, cbuf, dsend, drecv, dsum, xf, xb, mid, ybuf, yf,
                 x_ss, x_rs, xf_ss, xf_rs, g_ss, g_rs, f_ss, f_rs, s_ss, s_rs, sf_ss, sf_rs, d_ss, d_rs, e_ss, e_rs, p_ss, m_ss, m_rs, l_sem):
    row, col = lax.axis_index("row"), lax.axis_index("col")
    z, xh, k = row // 4, lax.rem(row // 2, 2), lax.rem(row, 2)
    y, xl = col // 2, lax.rem(col, 2)
    x = xh * 2 + xl

    def at4(v, s):
        return lax.rem(v + (s + 4), 4)

    def dev(x, y, z, k):
        return (z * 4 + (x // 2) * 2 + k, y * 2 + lax.rem(x, 2))

    x_dev = [dev(at4(x, r), y, z, k) for r in range(4)]
    y_dev = [dev(x, at4(y, 1), z, k), dev(x, at4(y, -1), z, k)]
    z_dev = [dev(x, y, at4(z, 1), k), dev(x, y, at4(z, -1), k)]
    sib = dev(x, y, z, 1 - k)
    turned = xl * 2 + xh
    m_dev = [dev(turned, z, y, k), dev(turned, z, y, 1 - k)]
    diagonal = y == z
    own_turned = jnp.logical_and(diagonal, xh == xl)

    bar = pltpu.get_barrier_semaphore()

    def greet(d):
        pl.semaphore_signal(bar, inc=1, device_id=d, device_id_type=MESH)

    for d in x_dev[1:] + y_dev + z_dev + [sib]:
        greet(d)

    @pl.when(diagonal)
    def _():
        greet(m_dev[1])
        for j in range(1, 4):
            for d in (dev(turned, at4(y, j), z, k), dev(turned, y, at4(z, j), 1 - k),
                      dev(x, y, at4(z, j), k), dev(x, at4(y, j), z, k)):
                greet(d)

        @pl.when(jnp.logical_not(own_turned))
        def _():
            greet(m_dev[0])

    @pl.when(jnp.logical_not(diagonal))
    def _():
        for d in (dev(turned, z, z, k), dev(turned, y, y, 1 - k), dev(x, y, y, k), dev(x, z, z, k), m_dev[0], m_dev[1]):
            greet(d)

    load_a = pltpu.make_async_copy(a_hbm, av, l_sem.at[0])
    load_w = pltpu.make_async_copy(w_hbm, wv, l_sem.at[1])
    load_w.start()
    load_a.start()

    def remote(src, dst, ss, rs, to):
        return pltpu.make_async_remote_copy(
            src_ref=src, dst_ref=dst, send_sem=ss, recv_sem=rs, device_id=to, device_id_type=MESH)

    def arrived(ref, ss, rs):
        remote(ref, ref, ss, rs, sib).wait_recv()

    sends = []

    def go(*args):
        copy = remote(*args)
        copy.start()
        sends.append(copy)

    q = lax.broadcasted_iota(jnp.int32, (PAIRS, PAIRS), 0)
    r = lax.broadcasted_iota(jnp.int32, (PAIRS, PAIRS), 1)
    perm = jnp.where(((q >> 4) == (r & 15)) & ((q & 15) == (r >> 4)), 1.0, 0.0).astype(BF16)

    def arrange_w(share, out):
        wp = jnp.dot(wv[pl.ds(share * 8, 8)].reshape(8 * BB, PAIRS), perm, preferred_element_type=F32)
        for h in range(2):
            for s in range(2):
                blocks = [wp[c8 * BB + s * 32:c8 * BB + s * 32 + 32, h * LANES:(h + 1) * LANES] for c8 in range(8)]
                for j8, v in enumerate(trade_chunks(blocks)):
                    at = (h * 8 + j8) * BB + s * 32
                    out[at:at + 32, :] = v.astype(BF16)

    def arrange_a(share, out):
        for lo in range(2):
            for h, wide in enumerate((wide0, wide1)):
                blocks = [wide[pl.ds((share + 4 * lo) * 8 + c8, BA, stride=BB), :] for c8 in range(8)]
                for i8, v in enumerate(trade_chunks(blocks)):
                    at = (h * 8 + i8) * 16
                    v = v.astype(BF16)
                    out[lo, at:at + 16, :] = v[:16]
                    out[lo, 256 + at:256 + at + 16, :] = v[16:]

    load_w.wait()
    arrange_w(x, wbuf.at[z, k, x])

    @pl.when(jnp.logical_not(diagonal))
    def _():
        pl.semaphore_wait(bar, 14)

    @pl.when(own_turned)
    def _():
        pl.semaphore_wait(bar, 21)

    @pl.when(jnp.logical_and(diagonal, xh != xl))
    def _():
        pl.semaphore_wait(bar, 22)

    def ring_w(r):
        src = at4(x, -r)
        if r == 2:
            for d in range(2):
                half = wbuf.at[z, k, src, pl.ds(d * 512, 512)]
                arrived(half, xf_ss.at[1, d], xf_rs.at[1, d])
        elif r:
            arrived(wbuf.at[z, k, src], x_ss.at[1, r], x_rs.at[1, r])
        for d in range(2):
            go(wbuf.at[z, k, src], wbuf.at[z, k, src], g_ss.at[1, d, r], g_rs.at[1, d, r], z_dev[d])
        go(wbuf.at[z, k, src], wbuf.at[z, k, src], s_ss.at[0, r], s_rs.at[0, r], sib)

    def ring_a(r):
        src = at4(x, -r)
        if r == 2:
            for d in range(2):
                arrived(abuf.at[y, src, d], xf_ss.at[0, d], xf_rs.at[0, d])
        elif r:
            arrived(abuf.at[y, src], x_ss.at[0, r], x_rs.at[0, r])
        for d in range(2):
            go(abuf.at[y, src], abuf.at[y, src], g_ss.at[0, d, r], g_rs.at[0, d, r], y_dev[d])

    beside = [x_dev[1], x_dev[3]]

    def near_w(n, _):
        r = 2 * n - 1
        to = at4(x, r)
        arrange_w(to, wtb.at[n])
        remote(wtb.at[n], wbuf.at[z, k, x], x_ss.at[1, r], x_rs.at[1, r], dev(to, y, z, k)).start()
        return 0

    def near_a(n, _):
        r = 2 * n - 1
        to = at4(x, r)
        arrange_a(to, atb.at[n])
        remote(atb.at[n], abuf.at[y, x], x_ss.at[0, r], x_rs.at[0, r], dev(to, y, z, k)).start()
        return 0

    def stage_w():
        for d in range(2):
            go(wtb.at[0, pl.ds(d * 512, 512)], rw.at[d], x_ss.at[1, 2 * d], x_rs.at[1, 2 * d], beside[d])

    def stage_a():
        for d in range(2):
            go(atb.at[0, d], ra.at[d], x_ss.at[0, 2 * d], x_rs.at[0, 2 * d], beside[d])

    def relay_w():
        for d in range(2):
            arrived(rw.at[d], x_ss.at[1, 2 * d], x_rs.at[1, 2 * d])
            go(rw.at[d], wbuf.at[z, k, at4(x, 2 * d - 1), pl.ds(d * 512, 512)], xf_ss.at[1, d], xf_rs.at[1, d], beside[d])

    def relay_a():
        for d in range(2):
            arrived(ra.at[d], x_ss.at[0, 2 * d], x_rs.at[0, 2 * d])
            go(ra.at[d], abuf.at[y, at4(x, 2 * d - 1), d], xf_ss.at[0, d], xf_rs.at[0, d], beside[d])

    def forward_w(r):
        src = at4(x, -r)
        for d in range(2):
            zz = at4(z, 2 * d - 1)
            arrived(wbuf.at[zz, k, src], g_ss.at[1, d, r], g_rs.at[1, d, r])
            half = wbuf.at[zz, k, src, pl.ds(d * 512, 512)]
            go(half, half, f_ss.at[1, d, r], f_rs.at[1, d, r], z_dev[d])
            go(wbuf.at[zz, k, src], wbuf.at[zz, k, src], s_ss.at[1 + d, r], s_rs.at[1 + d, r], sib)

    def forward_a(r):
        src = at4(x, -r)
        for d in range(2):
            yy = at4(y, 2 * d - 1)
            arrived(abuf.at[yy, src], g_ss.at[0, d, r], g_rs.at[0, d, r])
            go(abuf.at[yy, src, d], abuf.at[yy, src, d], f_ss.at[0, d, r], f_rs.at[0, d, r], y_dev[d])

    def finish_w(r):
        for d in range(2):
            half = wbuf.at[at4(z, 2), k, at4(x, -r), pl.ds(d * 512, 512)]
            arrived(half, f_ss.at[1, d, r], f_rs.at[1, d, r])
            go(half, half, sf_ss.at[d, r], sf_rs.at[d, r], sib)

    def finish_a(r):
        for d in range(2):
            arrived(abuf.at[at4(y, 2), at4(x, -r), d], f_ss.at[0, d, r], f_rs.at[0, d, r])

    ring_w(0)
    lax.fori_loop(1, 3, near_w, 0)
    load_a.wait()
    for h, wide in enumerate((wide0, wide1)):
        wide[...] = av[:, :, h * LANES:(h + 1) * LANES].astype(F32).reshape(BA * BB, LANES)
    arrange_a(x, abuf.at[y, x])
    ring_a(0)
    lax.fori_loop(1, 3, near_a, 0)
    arrange_w(at4(x, 2), wtb.at[0])
    arrange_a(at4(x, 2), atb.at[0])
    forward_w(0)
    ring_w(1)
    ring_w(3)
    stage_w()
    forward_a(0)
    ring_a(1)
    ring_a(3)
    stage_a()
    forward_w(1)
    relay_w()
    forward_a(1)
    relay_a()
    ring_w(2)
    forward_w(3)
    ring_a(2)
    forward_a(3)
    forward_w(2)
    forward_a(2)
    finish_w(0)
    finish_w(1)
    finish_w(3)
    finish_w(2)
    for r in (0, 1, 3, 2):
        finish_a(r)
    for r in range(4):
        src = at4(x, -r)
        arrived(wbuf.at[z, 1 - k, src], s_ss.at[0, r], s_rs.at[0, r])
        for d in range(2):
            zz = at4(z, 2 * d - 1)
            arrived(wbuf.at[zz, 1 - k, src], s_ss.at[1 + d, r], s_rs.at[1 + d, r])
            arrived(wbuf.at[at4(z, 2), 1 - k, src, pl.ds(d * 512, 512)], sf_ss.at[d, r], sf_rs.at[d, r])

    left = lax.broadcasted_iota(jnp.int32, (16, LANES), 1) < BB

    def quadrant(n, _):
        h, s = n // 4, lax.rem(n, 4)
        to = lax.rem(x + 2 - s + 3 * (s // 2) + 2 * (s // 3), 4)
        th, tl = to // 2, lax.rem(to, 2)
        split = [(hi, mid, lo) for hi in range(4) for mid in range(2) for lo in range(2)]

        def columns(n, _):
            rows = pl.ds(pl.multiple_of(h * 256, 256), 256)
            lhs = jnp.concatenate([abuf[hi, 2 * th + mid, lo, rows] for hi, mid, lo in split], axis=1)
            rhs = jnp.concatenate([wbuf[hi, lo, 2 * mid + tl, pl.ds(n, 1024)] for hi, mid, lo in split], axis=1)
            cbuf[...] = lax.dot_general(
                lhs, rhs, (((1,), (1,)), ((), ())), preferred_element_type=F32)
            return 0

        columns(0, 0)
        tiles = []
        for t, (i, jj) in enumerate(TILES):
            ii, ip = i // 2, i % 2
            here = cbuf[i * 16:(i + 1) * 16, jj * LANES:(jj + 1) * LANES]
            even = cbuf[2 * jj * 16:(2 * jj + 1) * 16, ii * LANES:(ii + 1) * LANES]
            odd = cbuf[(2 * jj + 1) * 16:(2 * jj + 2) * 16, ii * LANES:(ii + 1) * LANES]
            if ip == 0:
                other = jnp.where(left, even, pltpu.roll(odd, BB, 1))
            else:
                other = jnp.where(left, pltpu.roll(even, BB, 1), odd)
            tiles.append(here - other)
            if t % 2 == 0:
                continue
            for u in range(2):
                pair = jnp.concatenate([v[u * 8:u * 8 + 8] for v in tiles], axis=0)
                dsum[pl.ds((2 * h + u) * ROWS + (t - 1) * 8, 16), :] = pair
                dsend[n, u, (t - 1) * 8:(t + 1) * 8, :] = pair.astype(BF16)
            tiles = []

        @pl.when(s == 0)
        def _():
            stage_d(2 * h)

        @pl.when(lax.rem(s, 3) > 0)
        def _():
            near_d(2 * h, s)

        @pl.when(s == 3)
        def _():
            relay_d(2 * h)
            stage_d(2 * h + 1)
            near_d(2 * h + 1, 1)
            near_d(2 * h + 1, 2)

        @pl.when(n == 5)
        def _():
            relay_d(1)

        @pl.when(n == 6)
        def _():
            settle(0)
        return 0

    def term(c, s):
        return dsend.at[4 * (c // 2) + s, lax.rem(c, 2)]

    def d_copy(c, e, src, dst, to):
        return remote(src, dst, d_ss.at[c, e], d_rs.at[c, e], to)

    def stage_copy(c, d):
        return d_copy(c, d, term(c, 0).at[pl.ds(d * ROWS // 2, ROWS // 2)], rd.at[c, d], beside[d])

    def near_copy(c, s):
        return d_copy(c, s + 1, term(c, s), drecv.at[c, s], dev(at4(x, 3 - 2 * (2 - s)), y, z, k))

    def relay_copy(c, d):
        return d_copy(c, 4 + d, rd.at[c, d], drecv.at[c, 0, pl.ds(d * ROWS // 2, ROWS // 2)], beside[d])

    def stage_d(c):
        for d in range(2):
            stage_copy(c, d).start()

    def near_d(c, s):
        near_copy(c, s).start()

    def relay_d(c):
        for d in range(2):
            stage_copy(c, d).wait_recv()
            relay_copy(c, d).start()


    left2 = lax.broadcasted_iota(jnp.int32, (BB, LANES), 1) < BB

    def block(q, c):
        return xb.at[(k, 1 - k)[q], pl.ds(c * 8, 8)]

    def direct(q, c):
        return remote(block(q, c), ybuf.at[k, pl.ds(c * 8, 8)], m_ss.at[q, c], m_rs.at[q, c], m_dev[q])

    def same_chip(c):
        return pltpu.make_async_copy(block(0, c), ybuf.at[k, pl.ds(c * 8, 8)], l_sem.at[2 + c])

    def to_corner(q, c):
        if q == 0:
            corner, slot = dev(turned, z, z, k), lax.rem(y - z + 3, 4)
        else:
            corner, slot = dev(turned, y, y, 1 - k), lax.rem(z - y + 3, 4)
        return remote(block(q, c), mid.at[q, c, slot], e_ss.at[q, c], e_rs.at[q, c, slot], corner)

    def from_corner(q, c, j):
        there = dev(x, y, at4(z, 1 + j), k) if q == 0 else dev(x, at4(y, 1 + j), z, k)
        slot = k if q == 0 else 1 - k
        return remote(mid.at[q, c, j], ybuf.at[slot, pl.ds(c * 8, 8)], p_ss.at[q, c, j], m_rs.at[q, c], there)

    def pass_on(c):
        @pl.when(diagonal)
        def _():
            for q in range(2):
                if (q, c) in STRAIGHT:
                    continue

                def one(j, _):
                    arrived(mid.at[q, c, j], e_ss.at[q, c], e_rs.at[q, c, j])
                    from_corner(q, c, j).start()
                    return 0

                lax.fori_loop(0, 3, one, 0)

    def settle(c):
        for s in (1, 2):
            near_copy(c, s).wait_recv()
        for d in range(2):
            relay_copy(c, d).wait_recv()
        part = pl.ds(c * ROWS, ROWS)
        dsum[part, :] = dsum[part, :] + drecv[c, 0].astype(F32) + drecv[c, 1].astype(F32) + drecv[c, 2].astype(F32)

        def turn(p, _):
            rows = jnp.concatenate(
                [dsum[pl.ds(c * ROWS + 2 * p + q, NT, stride=8), :] for q in range(2)], axis=0)
            t = rows.T
            lo, hi = t[:BB], t[BB:]
            first = jnp.where(left2, lo, pltpu.roll(hi, BB, 1))
            second = jnp.where(left2, pltpu.roll(lo, BB, 1), hi)
            at = c * 8 + 2 * p
            xf[at] = first
            xf[at + 1] = second
            xb[0, at] = first[:BA].astype(BF16)
            xb[1, at] = first[BA:].astype(BF16)
            xb[0, at + 1] = second[:BA].astype(BF16)
            xb[1, at + 1] = second[BA:].astype(BF16)
            return 0

        lax.fori_loop(0, 4, turn, 0)

        @pl.when(jnp.logical_not(diagonal))
        def _():
            for q in range(2):
                (direct if (q, c) in STRAIGHT else to_corner)(q, c).start()

        @pl.when(diagonal)
        def _():
            direct(1, c).start()

            @pl.when(own_turned)
            def _():
                same_chip(c).start()

            @pl.when(jnp.logical_not(own_turned))
            def _():
                direct(0, c).start()


    lax.fori_loop(0, 8, quadrant, 0)
    relay_d(3)
    for c in range(1, 4):
        settle(c)
        pass_on(c - 1)
    pass_on(3)

    for c in range(4):
        @pl.when(own_turned)
        def _():
            same_chip(c).wait()

        @pl.when(jnp.logical_not(own_turned))
        def _():
            arrived(ybuf.at[k, pl.ds(c * 8, 8)], m_ss.at[0, c], m_rs.at[0, c])

        arrived(ybuf.at[1 - k, pl.ds(c * 8, 8)], m_ss.at[1, c], m_rs.at[1, c])
        for v in range(2):
            at = v * BA * BA + c * 8 * BA
            yf[at:at + 8 * BA, :] = ybuf[v, c * 8:c * 8 + 8].astype(F32).reshape(8 * BA, LANES)

    def mirror(a, _):
        r_ref[a] = xf[a] - yf[pl.ds(a, BB, stride=BA), :]
        return 0

    lax.fori_loop(0, BA, mirror, 0)
    for copy in sends:
        copy.wait_send()
    for n, r in ((1, 1), (2, 3)):
        remote(wtb.at[n], wbuf.at[z, k, x], x_ss.at[1, r], x_rs.at[1, r], sib).wait_send()
        remote(atb.at[n], abuf.at[y, x], x_ss.at[0, r], x_rs.at[0, r], sib).wait_send()
    for c in range(4):
        for s in (1, 2):
            near_copy(c, s).wait_send()
        for d in range(2):
            stage_copy(c, d).wait_send()
            relay_copy(c, d).wait_send()

        @pl.when(jnp.logical_not(diagonal))
        def _():
            for q in range(2):
                (direct if (q, c) in STRAIGHT else to_corner)(q, c).wait_send()

        @pl.when(diagonal)
        def _():
            direct(1, c).wait_send()
            for q in range(2):
                if (q, c) not in STRAIGHT:
                    for j in range(3):
                        from_corner(q, c, j).wait_send()

            @pl.when(jnp.logical_not(own_turned))
            def _():
                direct(0, c).wait_send()


STEP = 8


def update_kernel(a_ref, r_ref, sel_ref, occ_ref, vrow_ref, vcol_ref, o_ref):
    r = r_ref[...].reshape(STEP * BB, LANES)
    hi = r.astype(BF16)
    lo = (r - hi.astype(F32)).astype(BF16)
    full = jnp.dot(jnp.concatenate([hi, lo], axis=1), sel_ref[...], preferred_element_type=F32)
    lane = lax.broadcasted_iota(jnp.int32, (1, PAIRS), 1)
    occ_i, occ_j = jnp.zeros((1, PAIRS), F32), jnp.zeros((1, PAIRS), F32)
    for n in range(OCC):
        occ_i = jnp.where((lane >> 4) == n, occ_ref[n], occ_i)
        occ_j = jnp.where((lane & 15) == n, occ_ref[n], occ_j)
    den = ((occ_i + occ_j)[None] - vrow_ref[...]) - vcol_ref[...][None]
    o_ref[...] = a_ref[...].astype(F32) + full.reshape(STEP, BB, PAIRS) / den


def local(amplitudes, integrals, occ_energy, vir_energy):
    dma = pltpu.SemaphoreType.DMA
    resid = pl.pallas_call(
        cycle_kernel,
        out_shape=jax.ShapeDtypeStruct((BA, BB, LANES), F32),
        in_specs=[ANY, ANY],
        out_specs=VMEM,
        scratch_shapes=[
            pltpu.VMEM((BA, BB, PAIRS), BF16),
            pltpu.VMEM((BA, BB, PAIRS), BF16),
            pltpu.VMEM((BA * BB, LANES), F32),
            pltpu.VMEM((BA * BB, LANES), F32),
            pltpu.VMEM((3, 2, 512, LANES), BF16),
            pltpu.VMEM((3, 1024, LANES), BF16),
            pltpu.VMEM((2, 512, LANES), BF16),
            pltpu.VMEM((2, 512, LANES), BF16),
            pltpu.VMEM((4, 2, ROWS // 2, LANES), BF16),
            pltpu.VMEM((4, 4, 2, 512, LANES), BF16),
            pltpu.VMEM((4, 2, 4, 1024, LANES), BF16),
            pltpu.VMEM((256, 1024), F32),
            pltpu.VMEM((8, 2, ROWS, LANES), BF16),
            pltpu.VMEM((4, 3, ROWS, LANES), BF16),
            pltpu.VMEM((NT * BA, LANES), F32),
            pltpu.VMEM((BA, BB, LANES), F32),
            pltpu.VMEM((2, BA, BA, LANES), BF16),
            pltpu.VMEM((2, 4, 3, 8, BA, LANES), BF16),
            pltpu.VMEM((2, BA, BA, LANES), BF16),
            pltpu.VMEM((2 * BA * BA, LANES), F32),
            dma((2, 4)), dma((2, 4)), dma((2, 2)), dma((2, 2)), dma((2, 2, 4)), dma((2, 2, 4)), dma((2, 2, 4)), dma((2, 2, 4)),
            dma((3, 4)), dma((3, 4)), dma((2, 4)), dma((2, 4)), dma((4, 6)), dma((4, 6)),
            dma((2, 4)), dma((2, 4, 3)), dma((2, 4, 3)), dma((2, 4)), dma((2, 4)), dma((6,)),
        ],
        compiler_params=pltpu.CompilerParams(collective_id=0, has_side_effects=True, vmem_limit_bytes=48 << 20),
        name="cycle",
    )(amplitudes, integrals)
    row_pos, col_pos = lax.axis_index("row"), lax.axis_index("col")
    vir_rows = lax.dynamic_slice_in_dim(vir_energy, row_pos * BA, BA).reshape(BA, 1, 1)
    vir_cols = lax.dynamic_slice_in_dim(vir_energy, col_pos * BB, BB).reshape(BB, 1)
    sel = jnp.asarray(spread_matrix(), BF16)
    return pl.pallas_call(
        update_kernel,
        grid=(BA // STEP,),
        out_shape=jax.ShapeDtypeStruct((BA, BB, PAIRS), F32),
        in_specs=[
            pl.BlockSpec((STEP, BB, PAIRS), lambda s: (s, 0, 0)),
            pl.BlockSpec((STEP, BB, LANES), lambda s: (s, 0, 0)),
            pl.BlockSpec((2 * LANES, PAIRS), lambda s: (0, 0)),
            pl.BlockSpec(memory_space=pltpu.SMEM),
            pl.BlockSpec((STEP, 1, 1), lambda s: (s, 0, 0)),
            pl.BlockSpec((BB, 1), lambda s: (0, 0)),
        ],
        out_specs=pl.BlockSpec((STEP, BB, PAIRS), lambda s: (s, 0, 0)),
        compiler_params=pltpu.CompilerParams(vmem_limit_bytes=40 << 20),
        name="update",
    )(amplitudes, resid, sel, occ_energy, vir_rows, vir_cols)


def solution(mesh):
    placed = (P("row", "col", None), P("row", "col", None), P(), P())
    return jax.shard_map(
        local, mesh=mesh, in_specs=placed, out_specs=P("row", "col", None), check_vma=False
    )
```
